128 devices in a mesh: gx: 32 (over y, z, core), gy: 4 (over x).
Axes of the slice: x: 4, y: 4, z: 4, core: 2. Of those that a mesh axis runs over, the one named last changes fastest.
Arguments:
- latent: bfloat16 [256, 16, 128, 128], P('gx', 'gy'), may hold values from -6 to 6
- migration: int32 [32, 4, 8, 64], P('gx', 'gy'), may hold values from 0 to 4095, as said below
- tile_target: int32 [32, 4, 128], P('gx', 'gy'), may hold values from 0 to 31
- tile_offset: int32 [32, 4, 128], P('gx', 'gy'), may hold values from 0 to 8
- tile_count: int32 [32, 4], P('gx', 'gy'), may hold values from 64 to 128, as said below
- edge_sender: int32 [32, 4, 128, 128], P('gx', 'gy'), may hold values from 0 to 127
- edge_target: int32 [32, 4, 128, 128], P('gx', 'gy'), may hold values from 0 to 127
- send_weight: bfloat16 [3, 128, 128], replicated, may hold values from -0.375 to 0.375
- receive_weight: bfloat16 [3, 128, 128], replicated, may hold values from -0.375 to 0.375
- edge_bias: float32 [3, 128], replicated, may hold values from -3 to 3
- edge_weight: bfloat16 [3, 128, 128], replicated, may hold values from -0.5 to 0.5
- edge_gain: float32 [3, 128], replicated, may hold values from 0.5 to 2
- node_weight: bfloat16 [3, 128, 128], replicated, may hold values from -0.375 to 0.375
- aggregate_weight: bfloat16 [3, 128, 128], replicated, may hold values from -0.1875 to 0.1875
- node_bias: float32 [3, 128], replicated, may hold values from -3 to 3
- output_weight: bfloat16 [3, 128, 128], replicated, may hold values from -0.5 to 0.5
- node_gain: float32 [3, 128], replicated, may hold values from 0.5 to 2
Outputs:
- updated: bfloat16 [256, 16, 128, 128], P('gx', 'gy')
The draws below stay inside these ranges and needn't reach their ends.
Inputs may be any that keep to these rules, and one draw needn't show every extreme that they name: `migration`: within each device the 512 entries are distinct rows of 0 to 4095. `tile_count`: some device has all 128 tiles live.
All inputs are finite; a program needn't handle non-finite values.
Results may differ from the reference program's by a relative error of at most 0.009.
Values may be sent and summed in bfloat16 or wider, within the bound.
A program may use at most 128 MiB of HBM per device.

```python
import math
import jax
import jax.numpy as jnp
from jax import lax

D = 128
H = 128
BX = 8
BY = 4
SLOTS = 128
EDGES = 128
TILES = 128
MIG = 64
LAYERS = 3
DEV_X = 32
DEV_Y = 4
NBX = 256
NBY = 16


def draw_migration(key, part):
    key = jax.random.fold_in(key, 11)
    subkeys = jax.random.split(key, DEV_X * DEV_Y)
    total_rows = BX * BY * SLOTS

    def shuffle(subkey):
        return jax.random.permutation(subkey, total_rows)[:8 * MIG]
    shuffled = jax.vmap(shuffle)(subkeys)
    return shuffled.reshape(DEV_X, DEV_Y, 8, MIG).astype(jnp.int32)


def draw_tile_count(key, part):
    key = jax.random.fold_in(key, 12)
    first_key, second_key = jax.random.split(key)
    tile_counts = jax.random.randint(first_key, (DEV_X * DEV_Y,), TILES // 2, TILES + 1)
    busiest = jax.random.randint(second_key, (), 0, DEV_X * DEV_Y)
    tile_counts = tile_counts.at[busiest].set(TILES)
    return tile_counts.reshape(DEV_X, DEV_Y).astype(jnp.int32)


def set_ends(values, own_key, least, high):
    extent = values.shape
    index_at = [jax.random.randint(jax.random.fold_in(own_key, axis), (), 0, extent[axis]) for axis in range(len(extent))]
    values = values.at[tuple(index_at)].set(least)
    longest = extent.index(max(extent))
    index_at[longest] = (index_at[longest] + 1) % extent[longest]
    return values.at[tuple(index_at)].set(high)


def level_of(own_key, extent, cuts, smallest, high):
    def one(dim, blocks):
        heights = jax.random.uniform(jax.random.fold_in(jax.random.fold_in(own_key, 6), dim), (blocks,), jnp.float32, smallest / len(cuts), high / len(cuts))
        return jnp.repeat(jnp.exp(heights), extent[dim] // blocks).reshape((-1,) + (1,) * (len(extent) - dim - 1))

    level = one(*cuts[0])
    for cut in cuts[1:]:
        level = level * one(*cut)
    return level


def bell_draw(rng, extent, deviation, most, cuts=(), held_as=jnp.bfloat16):
    values = jax.random.normal(rng, extent, jnp.float32) * deviation
    if len(cuts) > 0:
        values = level_of(rng, extent, cuts, -0.22, 0.18) * values
    return jnp.clip(values, min=-most, max=most).astype(held_as)


def setup_inputs(seed: int = 0) -> dict:
    key_list = jax.random.split(jax.random.key(seed), 18)
    return {
        "latent": bell_draw(key_list[0], (NBX, NBY, SLOTS, D), 1.0, 6.0, ((0, 32), (1, 4))),
        "migration": draw_migration(jax.random.fold_in(key_list[17], 71), 0),
        "tile_target": set_ends(jax.random.randint(key_list[2], (DEV_X, DEV_Y, TILES), 0, BX * BY), jax.random.fold_in(key_list[2], 1), 0, (BX * BY) - 1).astype(jnp.int32),
        "tile_offset": set_ends(jax.random.randint(key_list[3], (DEV_X, DEV_Y, TILES), 0, 9), jax.random.fold_in(key_list[3], 1), 0, 8).astype(jnp.int32),
        "tile_count": draw_tile_count(jax.random.fold_in(key_list[17], 71), 0),
        "edge_sender": set_ends(jax.random.randint(key_list[5], (DEV_X, DEV_Y, TILES, EDGES), 0, SLOTS), jax.random.fold_in(key_list[5], 1), 0, SLOTS - 1).astype(jnp.int32),
        "edge_target": set_ends(jax.random.randint(key_list[6], (DEV_X, DEV_Y, TILES, EDGES), 0, SLOTS), jax.random.fold_in(key_list[6], 1), 0, SLOTS - 1).astype(jnp.int32),
        "send_weight": bell_draw(key_list[7], (LAYERS, D, H), (2 * D) ** -0.5, 0.375),
        "receive_weight": bell_draw(key_list[8], (LAYERS, D, H), (2 * D) ** -0.5, 0.375),
        "edge_bias": bell_draw(key_list[9], (LAYERS, H), 0.5, 3.0, (), jnp.float32),
        "edge_weight": bell_draw(key_list[10], (LAYERS, H, D), H ** -0.5, 0.5),
        "edge_gain": jnp.clip(jnp.exp(jax.random.uniform(key_list[11], (LAYERS, D), jnp.float32, math.log(0.5), math.log(2.0))), 0.5, 2.0),
        "node_weight": bell_draw(key_list[12], (LAYERS, D, H), (2 * D) ** -0.5, 0.375),
        "aggregate_weight": bell_draw(key_list[13], (LAYERS, D, H), (8 * D) ** -0.5, 0.1875),
        "node_bias": bell_draw(key_list[14], (LAYERS, H), 0.5, 3.0, (), jnp.float32),
        "output_weight": bell_draw(key_list[15], (LAYERS, H, D), H ** -0.5, 0.5),
        "node_gain": jnp.clip(jnp.exp(jax.random.uniform(key_list[16], (LAYERS, D), jnp.float32, math.log(0.5), math.log(2.0))), 0.5, 2.0),
    }


DIRECTIONS = ((-1, -1), (-1, 0), (-1, 1), (0, -1), (0, 1), (1, -1), (1, 0), (1, 1))

def layer_norm(values):
    average = lax.optimization_barrier(jnp.mean(values, axis=-1, keepdims=True))
    centred = values - average
    variance = lax.optimization_barrier(jnp.mean(centred * centred, axis=-1, keepdims=True))
    return centred * lax.rsqrt(variance + 1e-05)

def device_layer(extended, target_tiles, offsets, count, senders, receivers, weights):
    send_w, receive_w, edge_b, edge_w, edge_g, node_w, aggregate_w, node_b, output_w, node_g = weights
    bins_x = extended.shape[0] - 2
    bins_y = extended.shape[1] - 2
    bin_slots = extended.shape[2]
    features = extended.shape[3]
    extended_rows = extended.reshape(-1, bin_slots, features)
    resident = extended[1:-1, 1:-1].reshape(-1, features)
    sender_block = (target_tiles // bins_y + offsets // 3) * (bins_y + 2) + target_tiles % bins_y + offsets % 3
    sender_rows = extended_rows[sender_block[:, None], senders].reshape(-1, features)
    receiver_index = (target_tiles[:, None] * bin_slots + receivers).reshape(-1)
    receiver_rows = resident[receiver_index]
    hidden_pre = jnp.dot(sender_rows, send_w, preferred_element_type=jnp.float32)
    hidden_pre = hidden_pre + jnp.dot(receiver_rows, receive_w, preferred_element_type=jnp.float32) + edge_b
    edge_hidden = jax.nn.relu(hidden_pre).astype(jnp.bfloat16)
    edge_out = jnp.dot(edge_hidden, edge_w, preferred_element_type=jnp.float32)
    live_tiles = (jnp.arange(target_tiles.shape[0]) < count).astype(jnp.float32)
    live_edges = jnp.repeat(live_tiles, senders.shape[1])[:, None]
    messages = (layer_norm(edge_out) * edge_g * live_edges).astype(jnp.bfloat16)
    aggregate = jax.ops.segment_sum(messages.astype(jnp.float32), receiver_index, num_segments=resident.shape[0])
    node_pre = jnp.dot(resident, node_w, preferred_element_type=jnp.float32)
    node_pre = node_pre + jnp.dot(aggregate.astype(jnp.bfloat16), aggregate_w, preferred_element_type=jnp.float32) + node_b
    node_hidden = jax.nn.relu(node_pre).astype(jnp.bfloat16)
    node_out = jnp.dot(node_hidden, output_w, preferred_element_type=jnp.float32)
    renewed = (resident.astype(jnp.float32) + layer_norm(node_out) * node_g).astype(jnp.bfloat16)
    return renewed.reshape(bins_x, bins_y, bin_slots, features)

def pick_rows(particle_rows, leaving):
    return particle_rows[leaving]

def place_rows(particle_rows, target_rows, values):
    return particle_rows.at[target_rows].set(values)

def reference(latent, migration, tile_target, tile_offset, tile_count, edge_sender, edge_target, send_weight, receive_weight, edge_bias, edge_weight, edge_gain, node_weight, aggregate_weight, node_bias, output_weight, node_gain):
    features = latent.shape[3]
    device_count = DEV_X * DEV_Y
    blocked = latent.reshape(DEV_X, BX, DEV_Y, BY, SLOTS, features).transpose(0, 2, 1, 3, 4, 5)
    blocked = blocked.reshape(DEV_X, DEV_Y, BX * BY * SLOTS, features)
    moved = blocked
    for which, (step_x, step_y) in enumerate(DIRECTIONS):
        parcels = jax.vmap(jax.vmap(pick_rows))(blocked, migration[:, :, which])
        arrived = jnp.roll(parcels, (step_x, step_y), axis=(0, 1))
        moved = jax.vmap(jax.vmap(place_rows))(moved, migration[:, :, 7 - which], arrived)
    grid = moved.reshape(DEV_X, DEV_Y, BX, BY, SLOTS, features).transpose(0, 2, 1, 3, 4, 5)
    grid = grid.reshape(DEV_X * BX, DEV_Y * BY, SLOTS, features)
    targets = tile_target.reshape(device_count, -1)
    offsets = tile_offset.reshape(device_count, -1)
    counts = tile_count.reshape(device_count)
    senders = edge_sender.reshape(device_count, tile_target.shape[2], -1)
    receivers = edge_target.reshape(device_count, tile_target.shape[2], -1)
    device_ids = jnp.arange(device_count, dtype=jnp.int32)
    for layer_index in range(LAYERS):
        padded = jnp.pad(grid, ((1, 1), (1, 1), (0, 0), (0, 0)), mode='wrap')
        weights = tuple((array[layer_index] for array in (send_weight, receive_weight, edge_bias, edge_weight, edge_gain, node_weight, aggregate_weight, node_bias, output_weight, node_gain)))

        def one_device(inputs):
            device_id, target_tiles, tile_offsets, count, sender_slots, receiver_slots = inputs
            corner_x = device_id // DEV_Y * BX
            corner_y = device_id % DEV_Y * BY
            zero_index = jnp.zeros((), jnp.int32)
            extended = lax.dynamic_slice(padded, (corner_x, corner_y, zero_index, zero_index), (BX + 2, BY + 2, SLOTS, features))
            return device_layer(extended, target_tiles, tile_offsets, count, sender_slots, receiver_slots, weights)
        outcome = lax.map(one_device, (device_ids, targets, offsets, counts, senders, receivers))
        grid = outcome.reshape(DEV_X, DEV_Y, BX, BY, SLOTS, features).transpose(0, 2, 1, 3, 4, 5).reshape(grid.shape)
    return grid
```

```python
import jax
import jax.numpy as jnp
from jax import lax
from jax.experimental import pallas as pl
from jax.experimental.pallas import tpu as pltpu
from jax.sharding import PartitionSpec as P

DIRECTIONS = ((-1, -1), (-1, 0), (-1, 1), (0, -1), (0, 1), (1, -1), (1, 0), (1, 1))
MESH = pl.DeviceIdType.MESH
F32 = jnp.float32
BF16 = jnp.bfloat16
LANES = 128
GROUP = 16
LAYERS = 3


def dot(left, right):
    return jnp.dot(left, right, preferred_element_type=F32)


def turned(identity, block):
    return lax.dot_general(identity, block, (((1,), (1,)), ((), ())), preferred_element_type=F32)


def kernel(
    latent, mig_s, mig_v, target, offset, count, senders, receivers,
    send_w, recv_w, edge_b, edge_w, edge_g, node_w, agg_w, node_b, out_w, node_g,
    out_ref,
    lat, lat32, stage, parcels, arrived, arrived_t, mig_hot,
    es, er, hot, hot_n, ps0, ps1, ps2, pr, sums, state,
    w_sr, w_edge, w_node, w_out, columns, raw, plan_v, plan,
    in_sem, plan_sem, mig_send, mig_recv, halo_send, halo_recv, out_sem,
):
    bins_x, bins_y = out_ref.shape[0], out_ref.shape[1]
    tiles = es.shape[0]
    across = bins_x + 2
    tables = (ps0, ps1, ps2)
    a, b = lax.axis_index("gx"), lax.axis_index("gy")
    count_a, count_b = lax.axis_size("gx"), lax.axis_size("gy")

    def neighbour(step_x, step_y):
        return (lax.rem(a + step_x + count_a, count_a), lax.rem(b + step_y + count_b, count_b))

    lat_copy = pltpu.make_async_copy(latent, lat, in_sem.at[0])
    lat_copy.start()
    loads = [
        pltpu.make_async_copy(source, raw.at[which], in_sem.at[1 + which])
        for which, source in enumerate((send_w, recv_w, edge_w, node_w, agg_w, out_w))
    ]
    edge_loads = [
        pltpu.make_async_copy(senders.at[0, 0], es, in_sem.at[7]),
        pltpu.make_async_copy(receivers.at[0, 0], er, in_sem.at[8]),
    ]
    for copy in loads + edge_loads:
        copy.start()

    barrier = pltpu.get_barrier_semaphore()
    for step_x, step_y in DIRECTIONS:
        pl.semaphore_signal(
            barrier, inc=1, device_id=neighbour(step_x, step_y), device_id_type=MESH
        )

    lat_copy.wait()

    def widen(n, _):
        lat32[pl.ds(n * LANES, LANES), :] = lat[n // bins_y, n % bins_y].astype(F32)
        return 0

    lax.fori_loop(0, bins_x * bins_y, widen, 0, unroll=4)

    pl.semaphore_wait(barrier, 8)

    mig = mig_s.shape[3]
    mig_copies = []
    for which, (step_x, step_y) in enumerate(DIRECTIONS):

        def pick(m, _, which=which):
            stage[pl.ds(m, 1), :] = lat32[pl.ds(mig_s[0, 0, which, m], 1), :]
            return 0

        lax.fori_loop(0, mig, pick, 0, unroll=16)
        parcels[which] = stage[...].astype(BF16)
        copy = pltpu.make_async_remote_copy(
            src_ref=parcels.at[which],
            dst_ref=arrived.at[7 - which],
            send_sem=mig_send.at[which],
            recv_sem=mig_recv.at[7 - which],
            device_id=neighbour(step_x, step_y),
            device_id_type=MESH,
        )
        copy.start()
        mig_copies.append(copy)

    sub = lax.broadcasted_iota(jnp.int32, (LANES, LANES), 0)
    lane = lax.broadcasted_iota(jnp.int32, (LANES, LANES), 1)
    identity = jnp.where(sub == lane, 1.0, 0.0).astype(BF16)

    def spread(row):
        return jnp.transpose(jnp.broadcast_to(row, (LANES, LANES)))

    for quarter in range(4):
        row = jnp.concatenate(
            [mig_v[0, 0, 2 * quarter : 2 * quarter + 1, :], mig_v[0, 0, 2 * quarter + 1 : 2 * quarter + 2, :]],
            axis=1,
        ).astype(F32)
        index = spread(row).astype(jnp.int32)

        def mark(n, _, index=index, quarter=quarter):
            mig_hot[n, quarter * LANES : (quarter + 1) * LANES, :] = jnp.where(
                index - n * LANES == lane, 1.0, 0.0
            ).astype(BF16)
            return 0

        lax.fori_loop(0, bins_x * bins_y, mark, 0, unroll=4)

    def turn(n, _):
        state[n] = turned(identity, lat[n // bins_y, n % bins_y]).astype(BF16)
        return 0

    lax.fori_loop(0, bins_x * bins_y, turn, 0, unroll=8)

    lane_row = lax.broadcasted_iota(jnp.int32, (1, LANES), 1)
    bin_row = target[0, 0:1, :]
    off_row = offset[0, 0:1, :]
    step_row = jnp.right_shift(off_row * 11, 5)
    side_row = off_row - 3 * step_row
    sender_row = (jnp.bitwise_and(bin_row, 3) + side_row) * across + (
        jnp.right_shift(bin_row, 2) + step_row
    )
    key_row = bin_row * LANES + lane_row
    key_col = spread(key_row)
    packed_col = spread((sender_row * 32 + bin_row) * LANES + lane_row)
    rank = jnp.sum(
        jnp.where(jnp.broadcast_to(key_row, (LANES, LANES)) < key_col, 1, 0),
        axis=1,
        keepdims=True,
    )
    ordered = jnp.sum(jnp.where(rank == lane, packed_col, 0), axis=0, keepdims=True)
    tile_of = jnp.bitwise_and(ordered, LANES - 1)
    bin_of = jnp.bitwise_and(jnp.right_shift(ordered, 7), 31)
    sender_of = jnp.clip(jnp.right_shift(ordered, 12), 0, across * (bins_y + 2) - 1)
    before = pltpu.roll(bin_of, 1, 1)
    goes_on = jnp.where(jnp.logical_and(before == bin_of, lane_row > 0), 1, 0)
    live = jnp.where(tile_of < count[0, 0], 1, 0)
    bin_col = jnp.right_shift(key_col, 7)
    up_to = jnp.sum(jnp.where(bin_col <= lane, 1, 0), axis=0, keepdims=True)
    own = jnp.sum(jnp.where(bin_col == lane, 1, 0), axis=0, keepdims=True)
    last = jnp.clip(jnp.where(own > 0, up_to - 1, tiles), 0, tiles)
    plan_v[...] = jnp.concatenate(
        [tile_of, sender_of, bin_of, goes_on, live, last, last, last], axis=0
    )
    plan_copy = pltpu.make_async_copy(plan_v, plan, plan_sem)
    plan_copy.start()
    sums[tiles] = jnp.zeros((LANES, LANES), BF16)

    for copy in loads:
        copy.wait()
    for layer in range(LAYERS):
        w_sr[layer, :LANES, :] = turned(identity, raw[0, layer]).astype(BF16)
        w_sr[layer, LANES:, :] = turned(identity, raw[1, layer]).astype(BF16)
        for which, place in ((2, w_edge), (5, w_out)):
            full = turned(identity, raw[which, layer])
            place[layer] = (full - jnp.mean(full, axis=0, keepdims=True)).astype(BF16)
        w_node[layer, :, :LANES] = turned(identity, raw[3, layer]).astype(BF16)
        w_node[layer, :, LANES:] = (
            turned(identity, raw[4, layer]) * edge_g[layer : layer + 1, :]
        ).astype(BF16)
        columns[layer, 0] = spread(edge_b[layer : layer + 1, :])
        columns[layer, 1] = spread(node_b[layer : layer + 1, :])
        columns[layer, 2] = spread(node_g[layer : layer + 1, :])

    def place_tables(layer, cells, values):
        both = dot(w_sr[layer], values)
        for n, (i, j) in enumerate(cells):
            part = both[:, n * LANES : (n + 1) * LANES]
            tables[layer][(j + 1) * across + i + 1] = part[:LANES].astype(BF16)
            pr[i * bins_y + j] = (part[LANES:] + columns[layer, 0]).astype(BF16)

    def remote(layer, source, place, rows, slot, device):
        return pltpu.make_async_remote_copy(
            src_ref=tables[layer].at[pl.ds(source, rows)],
            dst_ref=tables[layer].at[pl.ds(place, rows)],
            send_sem=halo_send.at[layer, slot],
            recv_sem=halo_recv.at[layer, slot],
            device_id=device,
            device_id_type=MESH,
        )

    pairs = bins_x // 2

    def column_copies(layer, n):
        left = remote(
            layer, across + 1 + 2 * n, (bins_y + 1) * across + 1 + 2 * n, 2, n, neighbour(0, -1)
        )
        right = remote(
            layer, bins_y * across + 1 + 2 * n, 1 + 2 * n, 2, pairs + n, neighbour(0, 1)
        )
        return left, right

    def other_copies(layer):
        copies = []
        slot = 2 * pairs
        for step_x, step_y in ((-1, -1), (-1, 1), (1, -1), (1, 1)):
            source = (1 if step_y < 0 else bins_y) * across + (1 if step_x < 0 else bins_x)
            place = (bins_y + 1 if step_y < 0 else 0) * across + (
                bins_x + 1 if step_x < 0 else 0
            )
            copies.append(remote(layer, source, place, 1, slot, neighbour(step_x, step_y)))
            slot += 1
        for step_x in (-1, 1):
            for j in range(bins_y):
                source = (j + 1) * across + (1 if step_x < 0 else bins_x)
                place = (j + 1) * across + (bins_x + 1 if step_x < 0 else 0)
                copies.append(remote(layer, source, place, 1, slot, neighbour(step_x, 0)))
                slot += 1
        return copies

    def exchange(layer, renew):
        def outer(n, _):
            cells = [(2 * n, 0), (2 * n + 1, 0), (2 * n, bins_y - 1), (2 * n + 1, bins_y - 1)]
            place_tables(layer, cells, renew(cells))
            for copy in column_copies(layer, n):
                copy.start()
            return 0

        lax.fori_loop(0, pairs, outer, 0)
        corners = other_copies(layer)
        for copy in corners[:4]:
            copy.start()

        def inner(n, _):
            cells = [(2 * n, 1), (2 * n + 1, 1), (2 * n, 2), (2 * n + 1, 2)]
            place_tables(layer, cells, renew(cells))
            return 0

        lax.fori_loop(0, pairs, inner, 0)
        for copy in corners[4:]:
            copy.start()

    def finish_exchange(layer):
        for copy in other_copies(layer):
            copy.wait()
        for n in range(pairs):
            for copy in column_copies(layer, n):
                copy.wait()

    for copy in mig_copies:
        copy.wait()
    for quarter in range(4):
        block = jnp.concatenate([arrived[2 * quarter], arrived[2 * quarter + 1]], axis=0)
        arrived_t[:LANES, quarter * LANES : (quarter + 1) * LANES] = turned(
            identity, block
        ).astype(BF16)
    arrived_t[LANES:, :] = jnp.ones((16, 4 * LANES), BF16)

    def settle(cells):
        values = []
        for i, j in cells:
            n = i * bins_y + j
            placed = dot(arrived_t[...], mig_hot[n])
            new = jnp.where(
                placed[LANES : LANES + 1] > 0.5, placed[:LANES], state[n].astype(F32)
            ).astype(BF16)
            state[n] = new
            values.append(new)
        return jnp.concatenate(values, axis=1)

    exchange(0, settle)

    plan_copy.wait()
    for copy in edge_loads:
        copy.wait()

    def mark_tile(p, _):
        t = plan[0, p]
        from_row = es[pl.ds(t, 1), :]
        to_row = er[pl.ds(t, 1), :]
        hot[p, :LANES, :] = jnp.where(sub == from_row, 1.0, 0.0).astype(BF16)
        to_hot = jnp.where(sub == to_row, 1.0, 0.0).astype(BF16)
        hot[p, LANES:, :] = to_hot
        hot_n[p] = (turned(identity, to_hot) * plan[4, p].astype(F32)).astype(BF16)
        return 0

    lax.fori_loop(0, tiles, mark_tile, 0, unroll=8)

    def messages(layer):
        table = tables[layer]

        def group(q, total):
            hidden = []
            for g in range(GROUP):
                p = q * GROUP + g
                both = jnp.concatenate([table[plan[1, p]], pr[plan[2, p]]], axis=1)
                hidden.append(jnp.maximum(dot(both, hot[p]), 0.0).astype(BF16))
            sent = []
            for g in range(0, GROUP, 2):
                pair = dot(w_edge[layer], jnp.concatenate(hidden[g : g + 2], axis=1))
                var = jnp.mean(pair * pair, axis=0, keepdims=True)
                pair = (pair * lax.rsqrt(var + 1e-5)).astype(BF16)
                sent += [pair[:, :LANES], pair[:, LANES:]]
            for g in range(GROUP):
                p = q * GROUP + g
                total = total * plan[3, p].astype(F32) + dot(sent[g], hot_n[p])
                sums[p] = total.astype(BF16)
            return total

        lax.fori_loop(0, tiles // GROUP, group, jnp.zeros((LANES, LANES), F32))

    def node(layer):
        def renew(cells):
            old = jnp.concatenate([state[i * bins_y + j] for i, j in cells], axis=1)
            summed = jnp.concatenate(
                [sums[plan[5, i * bins_y + j]] for i, j in cells], axis=1
            )
            many = len(cells)
            bias = jnp.concatenate([columns[layer, 1]] * many, axis=1)
            gain = jnp.concatenate([columns[layer, 2]] * many, axis=1)
            hidden = dot(w_node[layer], jnp.concatenate([old, summed], axis=0)) + bias
            hidden = jnp.maximum(hidden, 0.0).astype(BF16)
            z = dot(w_out[layer], hidden)
            var = jnp.mean(z * z, axis=0, keepdims=True)
            new = (old.astype(F32) + z * lax.rsqrt(var + 1e-5) * gain).astype(BF16)
            if layer < LAYERS - 1:
                for n, (i, j) in enumerate(cells):
                    state[i * bins_y + j] = new[:, n * LANES : (n + 1) * LANES]
            return new

        return renew

    for layer in range(LAYERS):
        finish_exchange(layer)
        messages(layer)
        if layer < LAYERS - 1:
            exchange(layer + 1, node(layer))
        else:
            renew = node(layer)

            def final(n, _):
                cells = [(n, j) for j in range(bins_y)]
                new = renew(cells)
                for j in range(bins_y):
                    lat[n, j] = turned(identity, new[:, j * LANES : (j + 1) * LANES]).astype(BF16)
                pltpu.make_async_copy(lat.at[n], out_ref.at[n], out_sem.at[n]).start()
                return 0

            lax.fori_loop(0, bins_x, final, 0)
            for n in range(bins_x):
                pltpu.make_async_copy(lat.at[n], out_ref.at[n], out_sem.at[n]).wait()


def body(*arguments):
    latent, migration, tile_target, tile_offset, tile_count = arguments[:5]
    bins_x, bins_y, slots, features = latent.shape
    tiles = tile_target.shape[2]
    mig = migration.shape[3]
    cells = bins_x * bins_y
    table = (bins_x + 2) * (bins_y + 2)
    hbm = pl.BlockSpec(memory_space=pl.ANY)
    vmem = pl.BlockSpec(memory_space=pltpu.VMEM)
    smem = pl.BlockSpec(memory_space=pltpu.SMEM)
    block = (LANES, LANES)
    halos = 2 * (bins_x // 2) + 4 + 2 * bins_y
    dma = pltpu.SemaphoreType.DMA
    return pl.pallas_call(
        kernel,
        out_shape=jax.ShapeDtypeStruct(latent.shape, latent.dtype),
        in_specs=[
            hbm, smem, vmem, vmem, vmem, smem, hbm, hbm,
            hbm, hbm, vmem, hbm, vmem, hbm, hbm, vmem, hbm, vmem,
        ],
        out_specs=hbm,
        scratch_shapes=[
            pltpu.VMEM(latent.shape, BF16),
            pltpu.VMEM((cells * slots, features), F32),
            pltpu.VMEM((mig, features), F32),
            pltpu.VMEM((8, mig, features), BF16),
            pltpu.VMEM((8, mig, features), BF16),
            pltpu.VMEM((LANES + 16, 8 * mig), BF16),
            pltpu.VMEM((cells, 8 * mig, LANES), BF16),
            pltpu.VMEM((tiles, LANES), jnp.int32),
            pltpu.VMEM((tiles, LANES), jnp.int32),
            pltpu.VMEM((tiles, 2 * LANES, LANES), BF16),
            pltpu.VMEM((tiles,) + block, BF16),
            pltpu.VMEM((table,) + block, BF16),
            pltpu.VMEM((table,) + block, BF16),
            pltpu.VMEM((table,) + block, BF16),
            pltpu.VMEM((cells,) + block, BF16),
            pltpu.VMEM((tiles + 1,) + block, BF16),
            pltpu.VMEM((cells,) + block, BF16),
            pltpu.VMEM((LAYERS, 2 * LANES, LANES), BF16),
            pltpu.VMEM((LAYERS,) + block, BF16),
            pltpu.VMEM((LAYERS, LANES, 2 * LANES), BF16),
            pltpu.VMEM((LAYERS,) + block, BF16),
            pltpu.VMEM((LAYERS, 3) + block, F32),
            pltpu.VMEM((6, LAYERS) + block, BF16),
            pltpu.VMEM((8, LANES), jnp.int32),
            pltpu.SMEM((8, LANES), jnp.int32),
            dma((9,)),
            dma,
            dma((8,)),
            dma((8,)),
            dma((LAYERS, halos)),
            dma((LAYERS, halos)),
            dma((bins_x,)),
        ],
        compiler_params=pltpu.CompilerParams(
            collective_id=0, has_side_effects=True, vmem_limit_bytes=56 << 20
        ),
        name="particles",
    )(arguments[0], migration, *arguments[1:])


def solution(mesh):
    split = P("gx", "gy")
    in_specs = (split,) * 7 + (P(),) * 10
    return jax.shard_map(
        body, mesh=mesh, in_specs=in_specs, out_specs=split, check_vma=False
    )
```

```python
import jax
import jax.numpy as jnp
from jax import lax
from jax.experimental import pallas as pl
from jax.experimental.pallas import tpu as pltpu
from jax.sharding import PartitionSpec as P

DIRECTIONS = ((-1, -1), (-1, 0), (-1, 1), (0, -1), (0, 1), (1, -1), (1, 0), (1, 1))
MESH = pl.DeviceIdType.MESH
F32 = jnp.float32
BF16 = jnp.bfloat16
LANES = 128
GROUP = 32
LAYERS = 3
EARLY = 64
FINAL = 4


def dot(left, right):
    return jnp.dot(left, right, preferred_element_type=F32)


def turned(identity, block):
    return lax.dot_general(identity, block, (((1,), (1,)), ((), ())), preferred_element_type=F32)


def kernel(
    latent, mig_s, mig_v, target, offset, count, senders, receivers,
    send_w, recv_w, edge_b, edge_w, edge_g, node_w, agg_w, node_b, out_w, node_g,
    out_ref,
    lat, lat32, stage, parcels, arrived, arrived_t, mig_hot,
    es, er, hot, hot_n, to_rows, ps0, ps1, ps2, pr, sums, state,
    w_sr, w_edge, w_node, w_out, columns, raw, plan_v, plan,
    in_sem, plan_sem, mig_send, mig_recv, halo_send, halo_recv, out_sem,
):
    bins_x, bins_y = out_ref.shape[0], out_ref.shape[1]
    tiles = es.shape[0]
    across = bins_x + 2
    tables = (ps0, ps1, ps2)
    a, b = lax.axis_index("gx"), lax.axis_index("gy")
    count_a, count_b = lax.axis_size("gx"), lax.axis_size("gy")

    def neighbour(step_x, step_y):
        return (lax.rem(a + step_x + count_a, count_a), lax.rem(b + step_y + count_b, count_b))

    lat_copy = pltpu.make_async_copy(latent, lat, in_sem.at[0])
    lat_copy.start()
    loads = [
        pltpu.make_async_copy(source, raw.at[which], in_sem.at[1 + which])
        for which, source in enumerate((send_w, recv_w, edge_w, node_w, agg_w, out_w))
    ]
    edge_loads = [
        pltpu.make_async_copy(senders.at[0, 0], es, in_sem.at[7]),
        pltpu.make_async_copy(receivers.at[0, 0], er, in_sem.at[8]),
    ]
    for copy in loads + edge_loads:
        copy.start()

    barrier = pltpu.get_barrier_semaphore()
    for step_x, step_y in DIRECTIONS:
        pl.semaphore_signal(
            barrier, inc=1, device_id=neighbour(step_x, step_y), device_id_type=MESH
        )

    lat_copy.wait()

    def widen(n, _):
        lat32[pl.ds(n * LANES, LANES), :] = lat[n // bins_y, n % bins_y].astype(F32)
        return 0

    lax.fori_loop(0, bins_x * bins_y, widen, 0, unroll=4)

    pl.semaphore_wait(barrier, 8)

    mig = mig_s.shape[3]
    mig_copies = []
    for which, (step_x, step_y) in enumerate(DIRECTIONS):

        def pick(m, _, which=which):
            stage[pl.ds(m, 1), :] = lat32[pl.ds(mig_s[0, 0, which, m], 1), :]
            return 0

        lax.fori_loop(0, mig, pick, 0, unroll=16)
        parcels[which] = stage[...].astype(BF16)
        copy = pltpu.make_async_remote_copy(
            src_ref=parcels.at[which],
            dst_ref=arrived.at[7 - which],
            send_sem=mig_send.at[which],
            recv_sem=mig_recv.at[7 - which],
            device_id=neighbour(step_x, step_y),
            device_id_type=MESH,
        )
        copy.start()
        mig_copies.append(copy)

    sub = lax.broadcasted_iota(jnp.int32, (LANES, LANES), 0)
    lane = lax.broadcasted_iota(jnp.int32, (LANES, LANES), 1)
    identity = jnp.where(sub == lane, 1.0, 0.0).astype(BF16)

    def spread(row):
        return jnp.transpose(jnp.broadcast_to(row, (LANES, LANES)))

    for quarter in range(4):
        row = jnp.concatenate(
            [mig_v[0, 0, 2 * quarter : 2 * quarter + 1, :], mig_v[0, 0, 2 * quarter + 1 : 2 * quarter + 2, :]],
            axis=1,
        ).astype(F32)
        index = spread(row).astype(jnp.int32)

        def mark(n, _, index=index, quarter=quarter):
            mig_hot[n, quarter * LANES : (quarter + 1) * LANES, :] = jnp.where(
                index - n * LANES == lane, 1.0, 0.0
            ).astype(BF16)
            return 0

        lax.fori_loop(0, bins_x * bins_y, mark, 0, unroll=4)

    def turn(n, _):
        state[n] = turned(identity, lat[n // bins_y, n % bins_y]).astype(BF16)
        return 0

    lax.fori_loop(0, bins_x * bins_y, turn, 0, unroll=8)

    lane_row = lax.broadcasted_iota(jnp.int32, (1, LANES), 1)
    bin_row = target[0, 0:1, :]
    off_row = offset[0, 0:1, :]
    step_row = jnp.right_shift(off_row * 11, 5)
    side_row = off_row - 3 * step_row
    sender_row = (jnp.bitwise_and(bin_row, 3) + side_row) * 16 + (
        jnp.right_shift(bin_row, 2) + step_row
    )
    key_row = bin_row * LANES + lane_row
    key_col = spread(key_row)
    packed_col = spread((sender_row * 32 + bin_row) * LANES + lane_row)
    rank = jnp.sum(
        jnp.where(jnp.broadcast_to(key_row, (LANES, LANES)) < key_col, 1, 0),
        axis=1,
        keepdims=True,
    )
    ordered = jnp.sum(jnp.where(rank == lane, packed_col, 0), axis=0, keepdims=True)
    tile_of = jnp.bitwise_and(ordered, LANES - 1)
    bin_of = jnp.bitwise_and(jnp.right_shift(ordered, 7), 31)
    sender_y = jnp.clip(jnp.right_shift(ordered, 16), 0, bins_y + 1)
    sender_x = jnp.clip(jnp.bitwise_and(jnp.right_shift(ordered, 12), 15), 0, across - 1)
    before = pltpu.roll(bin_of, 1, 1)
    goes_on = jnp.where(jnp.logical_and(before == bin_of, lane_row > 0), 1, 0)
    live = jnp.where(tile_of < count[0, 0], 1, 0)
    bin_col = jnp.right_shift(key_col, 7)
    up_to = jnp.sum(jnp.where(bin_col <= lane, 1, 0), axis=0, keepdims=True)
    own = jnp.sum(jnp.where(bin_col == lane, 1, 0), axis=0, keepdims=True)
    last = jnp.clip(jnp.where(own > 0, up_to - 1, tiles), 0, tiles)
    plan_v[...] = jnp.concatenate(
        [tile_of, sender_y, bin_of, goes_on, live, last, sender_x, last], axis=0
    )
    plan_copy = pltpu.make_async_copy(plan_v, plan, plan_sem)
    plan_copy.start()
    sums[tiles] = jnp.zeros((LANES, LANES), BF16)

    for copy in loads:
        copy.wait()
    for layer in range(LAYERS):
        w_sr[layer, :LANES, :] = turned(identity, raw[0, layer]).astype(BF16)
        w_sr[layer, LANES:, :] = turned(identity, raw[1, layer]).astype(BF16)
        for which, place in ((2, w_edge), (5, w_out)):
            full = turned(identity, raw[which, layer])
            place[layer] = (full - jnp.mean(full, axis=0, keepdims=True)).astype(BF16)
        w_node[layer, :, :LANES] = turned(identity, raw[3, layer]).astype(BF16)
        w_node[layer, :, LANES:] = (
            turned(identity, raw[4, layer]) * edge_g[layer : layer + 1, :]
        ).astype(BF16)
        columns[layer, 0] = spread(edge_b[layer : layer + 1, :])
        columns[layer, 1] = spread(node_b[layer : layer + 1, :])
        columns[layer, 2] = spread(node_g[layer : layer + 1, :])

    def place_tables(layer, cells, values):
        both = dot(w_sr[layer], values)
        for n, (i, j) in enumerate(cells):
            part = both[:, n * LANES : (n + 1) * LANES]
            tables[layer][j + 1, i + 1] = part[:LANES].astype(BF16)
            pr[i * bins_y + j] = (part[LANES:] + columns[layer, 0]).astype(BF16)

    def remote(layer, source, place, which):
        return pltpu.make_async_remote_copy(
            src_ref=tables[layer].at[source],
            dst_ref=tables[layer].at[place],
            send_sem=halo_send.at[layer, which],
            recv_sem=halo_recv.at[layer, which],
            device_id=neighbour(*DIRECTIONS[which]),
            device_id_type=MESH,
        )

    def halo(layer, which, rows=None):
        step_x, step_y = DIRECTIONS[which]
        near_y, far_y = (1, bins_y + 1) if step_y < 0 else (bins_y, 0)
        near_x, far_x = (1, bins_x + 1) if step_x < 0 else (bins_x, 0)
        if step_x == 0:
            rows = pl.ds(1, bins_x) if rows is None else rows
            return remote(layer, (near_y, rows), (far_y, rows), which)
        if step_y == 0:
            columns_ = pl.ds(1, bins_y)
            return remote(layer, (columns_, near_x), (columns_, far_x), which)
        return remote(layer, (near_y, near_x), (far_y, far_x), which)

    def exchange(layer, renew):
        left, right, low, high = 0, bins_y - 1, 0, bins_x - 1
        cells = [(low, left), (high, left), (low, right), (high, right)]
        place_tables(layer, cells, renew(cells))
        for which in (0, 2, 5, 7):
            halo(layer, which).start()
        for which in (3, 4):
            halo(layer, which, pl.ds(1 + low, 1)).start()
            halo(layer, which, pl.ds(1 + high, 1)).start()
        cells = [(i, j) for i in (low, high) for j in range(left + 1, right)]
        place_tables(layer, cells, renew(cells))
        for which in (1, 6):
            halo(layer, which).start()

        def outer(n, _):
            row = 2 * n + 1
            cells = [(row, left), (row + 1, left), (row, right), (row + 1, right)]
            place_tables(layer, cells, renew(cells))
            for which in (3, 4):
                halo(layer, which, pl.ds(1 + row, 2)).start()
            return 0

        lax.fori_loop(0, bins_x // 2 - 1, outer, 0)

        def inner(n, _):
            row = 2 * n + 1
            cells = [(row + i, j) for i in range(2) for j in range(left + 1, right)]
            place_tables(layer, cells, renew(cells))
            return 0

        lax.fori_loop(0, bins_x // 2 - 1, inner, 0)

    def finish_exchange(layer):
        for which in range(8):
            halo(layer, which).wait_recv()

    plan_copy.wait()
    for copy in edge_loads:
        copy.wait()

    def mark_tile(p, _):
        t = plan[0, p]
        from_row = es[pl.ds(t, 1), :]
        to_row = er[pl.ds(t, 1), :]
        hot[p, :LANES, :] = jnp.where(sub == from_row, 1.0, 0.0).astype(BF16)
        to_hot = jnp.where(sub == to_row, 1.0, 0.0).astype(BF16)
        hot[p, LANES:, :] = to_hot
        hot_n[p] = (turned(identity, to_hot) * plan[4, p].astype(F32)).astype(BF16)
        return 0

    lax.fori_loop(0, EARLY, mark_tile, 0, unroll=8)

    for copy in mig_copies:
        copy.wait()
    for quarter in range(4):
        block = jnp.concatenate([arrived[2 * quarter], arrived[2 * quarter + 1]], axis=0)
        arrived_t[:LANES, quarter * LANES : (quarter + 1) * LANES] = turned(
            identity, block
        ).astype(BF16)
    arrived_t[LANES:, :] = jnp.ones((16, 4 * LANES), BF16)

    def settle(cells):
        values = []
        for i, j in cells:
            n = i * bins_y + j
            placed = dot(arrived_t[...], mig_hot[n])
            new = jnp.where(
                placed[LANES : LANES + 1] > 0.5, placed[:LANES], state[n].astype(F32)
            ).astype(BF16)
            state[n] = new
            values.append(new)
        return jnp.concatenate(values, axis=1)

    exchange(0, settle)
    lax.fori_loop(EARLY, tiles, mark_tile, 0, unroll=8)

    def receivers_of(p, _):
        to_rows[p] = dot(pr[plan[2, p]], hot[p, LANES:, :]).astype(BF16)
        return 0

    def messages(layer):
        table = tables[layer]

        def group(q, total):
            hidden = []
            for g in range(GROUP):
                p = q * GROUP + g
                pre = dot(table[plan[1, p], plan[6, p]], hot[p, :LANES, :])
                hidden.append(jnp.maximum(pre + to_rows[p].astype(F32), 0.0).astype(BF16))
            sent = []
            for g in range(0, GROUP, 2):
                pair = dot(w_edge[layer], jnp.concatenate(hidden[g : g + 2], axis=1))
                var = jnp.mean(pair * pair, axis=0, keepdims=True)
                pair = (pair * lax.rsqrt(var + 1e-5)).astype(BF16)
                sent += [pair[:, :LANES], pair[:, LANES:]]
            for g in range(GROUP):
                p = q * GROUP + g
                total = total * plan[3, p].astype(F32) + dot(sent[g], hot_n[p])
                sums[p] = total.astype(BF16)
            return total

        lax.fori_loop(0, tiles // GROUP, group, jnp.zeros((LANES, LANES), F32))

    def node(layer):
        def renew(cells):
            old = jnp.concatenate([state[i * bins_y + j] for i, j in cells], axis=1)
            summed = jnp.concatenate(
                [sums[plan[5, i * bins_y + j]] for i, j in cells], axis=1
            )
            many = len(cells)
            bias = jnp.concatenate([columns[layer, 1]] * many, axis=1)
            gain = jnp.concatenate([columns[layer, 2]] * many, axis=1)
            hidden = dot(w_node[layer], jnp.concatenate([old, summed], axis=0)) + bias
            hidden = jnp.maximum(hidden, 0.0).astype(BF16)
            z = dot(w_out[layer], hidden)
            var = jnp.mean(z * z, axis=0, keepdims=True)
            new = (old.astype(F32) + z * lax.rsqrt(var + 1e-5) * gain).astype(BF16)
            if layer < LAYERS - 1:
                for n, (i, j) in enumerate(cells):
                    state[i * bins_y + j] = new[:, n * LANES : (n + 1) * LANES]
            return new

        return renew

    for layer in range(LAYERS):
        lax.fori_loop(0, tiles, receivers_of, 0, unroll=16)
        finish_exchange(layer)
        messages(layer)
        if layer < LAYERS - 1:
            exchange(layer + 1, node(layer))
        else:
            renew = node(layer)

            def final(n, _):
                cells = [(FINAL * n + i, j) for i in range(FINAL) for j in range(bins_y)]
                new = renew(cells)
                for k, (i, j) in enumerate(cells):
                    lat[i, j] = turned(identity, new[:, k * LANES : (k + 1) * LANES]).astype(BF16)
                rows = pl.ds(FINAL * n, FINAL)
                pltpu.make_async_copy(lat.at[rows], out_ref.at[rows], out_sem.at[n]).start()
                return 0

            lax.fori_loop(0, bins_x // FINAL, final, 0)
            for n in range(bins_x // FINAL):
                rows = pl.ds(FINAL * n, FINAL)
                pltpu.make_async_copy(lat.at[rows], out_ref.at[rows], out_sem.at[n]).wait()
    for layer in range(LAYERS):
        for which in range(8):
            halo(layer, which).wait_send()


def body(*arguments):
    latent, migration, tile_target, tile_offset, tile_count = arguments[:5]
    bins_x, bins_y, slots, features = latent.shape
    tiles = tile_target.shape[2]
    mig = migration.shape[3]
    cells = bins_x * bins_y
    table = (bins_y + 2, bins_x + 2)
    hbm = pl.BlockSpec(memory_space=pl.ANY)
    vmem = pl.BlockSpec(memory_space=pltpu.VMEM)
    smem = pl.BlockSpec(memory_space=pltpu.SMEM)
    block = (LANES, LANES)
    dma = pltpu.SemaphoreType.DMA
    return pl.pallas_call(
        kernel,
        out_shape=jax.ShapeDtypeStruct(latent.shape, latent.dtype),
        in_specs=[
            hbm, smem, vmem, vmem, vmem, smem, hbm, hbm,
            hbm, hbm, vmem, hbm, vmem, hbm, hbm, vmem, hbm, vmem,
        ],
        out_specs=hbm,
        scratch_shapes=[
            pltpu.VMEM(latent.shape, BF16),
            pltpu.VMEM((cells * slots, features), F32),
            pltpu.VMEM((mig, features), F32),
            pltpu.VMEM((8, mig, features), BF16),
            pltpu.VMEM((8, mig, features), BF16),
            pltpu.VMEM((LANES + 16, 8 * mig), BF16),
            pltpu.VMEM((cells, 8 * mig, LANES), BF16),
            pltpu.VMEM((tiles, LANES), jnp.int32),
            pltpu.VMEM((tiles, LANES), jnp.int32),
            pltpu.VMEM((tiles, 2 * LANES, LANES), BF16),
            pltpu.VMEM((tiles,) + block, BF16),
            pltpu.VMEM((tiles,) + block, BF16),
            pltpu.VMEM(table + block, BF16),
            pltpu.VMEM(table + block, BF16),
            pltpu.VMEM(table + block, BF16),
            pltpu.VMEM((cells,) + block, BF16),
            pltpu.VMEM((tiles + 1,) + block, BF16),
            pltpu.VMEM((cells,) + block, BF16),
            pltpu.VMEM((LAYERS, 2 * LANES, LANES), BF16),
            pltpu.VMEM((LAYERS,) + block, BF16),
            pltpu.VMEM((LAYERS, LANES, 2 * LANES), BF16),
            pltpu.VMEM((LAYERS,) + block, BF16),
            pltpu.VMEM((LAYERS, 3) + block, F32),
            pltpu.VMEM((6, LAYERS) + block, BF16),
            pltpu.VMEM((8, LANES), jnp.int32),
            pltpu.SMEM((8, LANES), jnp.int32),
            dma((9,)),
            dma,
            dma((8,)),
            dma((8,)),
            dma((LAYERS, 8)),
            dma((LAYERS, 8)),
            dma((bins_x,)),
        ],
        compiler_params=pltpu.CompilerParams(
            collective_id=0, has_side_effects=True, vmem_limit_bytes=56 << 20
        ),
        name="particles",
    )(arguments[0], migration, *arguments[1:])


def solution(mesh):
    split = P("gx", "gy")
    in_specs = (split,) * 7 + (P(),) * 10
    return jax.shard_map(
        body, mesh=mesh, in_specs=in_specs, out_specs=split, check_vma=False
    )
```

```python
import jax
import jax.numpy as jnp
from jax import lax
from jax.experimental import pallas as pl
from jax.experimental.pallas import tpu as pltpu
from jax.sharding import PartitionSpec as P

DIRECTIONS = ((-1, -1), (-1, 0), (-1, 1), (0, -1), (0, 1), (1, -1), (1, 0), (1, 1))
MESH = pl.DeviceIdType.MESH
F32 = jnp.float32
BF16 = jnp.bfloat16
LANES = 128
GROUP = 64
LAYERS = 3
EARLY = 64
FINAL = 4


def dot(left, right):
    return jnp.dot(left, right, preferred_element_type=F32)


def turned(identity, block):
    return lax.dot_general(identity, block, (((1,), (1,)), ((), ())), preferred_element_type=F32)


def kernel(
    latent, mig_s, mig_v, target, offset, count, senders, receivers,
    send_w, recv_w, edge_b, edge_w, edge_g, node_w, agg_w, node_b, out_w, node_g,
    out_ref,
    lat, lat32, stage, parcels, arrived, arrived_t, mig_hot,
    es, er, hot, hot_n, to_rows, ps0, ps1, ps2, pr, sums, state,
    w_sr, w_edge, w_node, w_out, columns, raw, plan_v, plan,
    in_sem, plan_sem, mig_send, mig_recv, halo_send, halo_recv, out_sem,
):
    bins_x, bins_y = out_ref.shape[0], out_ref.shape[1]
    tiles = es.shape[0]
    across = bins_x + 2
    tables = (ps0, ps1, ps2)
    a, b = lax.axis_index("gx"), lax.axis_index("gy")
    count_a, count_b = lax.axis_size("gx"), lax.axis_size("gy")

    def neighbour(step_x, step_y):
        return (lax.rem(a + step_x + count_a, count_a), lax.rem(b + step_y + count_b, count_b))

    lat_copy = pltpu.make_async_copy(latent, lat, in_sem.at[0])
    lat_copy.start()
    loads = [
        pltpu.make_async_copy(source, raw.at[which], in_sem.at[1 + which])
        for which, source in enumerate((send_w, recv_w, edge_w, node_w, agg_w, out_w))
    ]
    edge_loads = [
        pltpu.make_async_copy(senders.at[0, 0], es, in_sem.at[7]),
        pltpu.make_async_copy(receivers.at[0, 0], er, in_sem.at[8]),
    ]
    for copy in loads + edge_loads:
        copy.start()

    barrier = pltpu.get_barrier_semaphore()
    for step_x, step_y in DIRECTIONS:
        pl.semaphore_signal(
            barrier, inc=1, device_id=neighbour(step_x, step_y), device_id_type=MESH
        )

    lat_copy.wait()

    def widen(n, _):
        lat32[pl.ds(n * LANES, LANES), :] = lat[n // bins_y, n % bins_y].astype(F32)
        return 0

    lax.fori_loop(0, bins_x * bins_y, widen, 0, unroll=4)

    pl.semaphore_wait(barrier, 8)

    mig = mig_s.shape[3]
    mig_copies = []
    for which, (step_x, step_y) in enumerate(DIRECTIONS):

        def pick(m, _, which=which):
            stage[pl.ds(m, 1), :] = lat32[pl.ds(mig_s[0, 0, which, m], 1), :]
            return 0

        lax.fori_loop(0, mig, pick, 0, unroll=16)
        parcels[which] = stage[...].astype(BF16)
        copy = pltpu.make_async_remote_copy(
            src_ref=parcels.at[which],
            dst_ref=arrived.at[7 - which],
            send_sem=mig_send.at[which],
            recv_sem=mig_recv.at[7 - which],
            device_id=neighbour(step_x, step_y),
            device_id_type=MESH,
        )
        copy.start()
        mig_copies.append(copy)

    sub = lax.broadcasted_iota(jnp.int32, (LANES, LANES), 0)
    lane = lax.broadcasted_iota(jnp.int32, (LANES, LANES), 1)
    identity = jnp.where(sub == lane, 1.0, 0.0).astype(BF16)

    def spread(row):
        return jnp.transpose(jnp.broadcast_to(row, (LANES, LANES)))

    for quarter in range(4):
        row = jnp.concatenate(
            [mig_v[0, 0, 2 * quarter : 2 * quarter + 1, :], mig_v[0, 0, 2 * quarter + 1 : 2 * quarter + 2, :]],
            axis=1,
        ).astype(F32)
        index = spread(row).astype(jnp.int32)

        def mark(n, _, index=index, quarter=quarter):
            mig_hot[n, quarter * LANES : (quarter + 1) * LANES, :] = jnp.where(
                index - n * LANES == lane, 1.0, 0.0
            ).astype(BF16)
            return 0

        lax.fori_loop(0, bins_x * bins_y, mark, 0, unroll=4)

    def turn(n, _):
        state[n] = turned(identity, lat[n // bins_y, n % bins_y]).astype(BF16)
        return 0

    lax.fori_loop(0, bins_x * bins_y, turn, 0, unroll=8)

    lane_row = lax.broadcasted_iota(jnp.int32, (1, LANES), 1)
    bin_row = target[0, 0:1, :]
    off_row = offset[0, 0:1, :]
    step_row = jnp.right_shift(off_row * 11, 5)
    side_row = off_row - 3 * step_row
    sender_row = (jnp.bitwise_and(bin_row, 3) + side_row) * 16 + (
        jnp.right_shift(bin_row, 2) + step_row
    )
    key_row = bin_row * LANES + lane_row
    key_col = spread(key_row)
    packed_col = spread((sender_row * 32 + bin_row) * LANES + lane_row)
    rank = jnp.sum(
        jnp.where(jnp.broadcast_to(key_row, (LANES, LANES)) < key_col, 1, 0),
        axis=1,
        keepdims=True,
    )
    ordered = jnp.sum(jnp.where(rank == lane, packed_col, 0), axis=0, keepdims=True)
    tile_of = jnp.bitwise_and(ordered, LANES - 1)
    bin_of = jnp.bitwise_and(jnp.right_shift(ordered, 7), 31)
    sender_y = jnp.clip(jnp.right_shift(ordered, 16), 0, bins_y + 1)
    sender_x = jnp.clip(jnp.bitwise_and(jnp.right_shift(ordered, 12), 15), 0, across - 1)
    before = pltpu.roll(bin_of, 1, 1)
    goes_on = jnp.where(jnp.logical_and(before == bin_of, lane_row > 0), 1, 0)
    live = jnp.where(tile_of < count[0, 0], 1, 0)
    bin_col = jnp.right_shift(key_col, 7)
    up_to = jnp.sum(jnp.where(bin_col <= lane, 1, 0), axis=0, keepdims=True)
    own = jnp.sum(jnp.where(bin_col == lane, 1, 0), axis=0, keepdims=True)
    last = jnp.clip(jnp.where(own > 0, up_to - 1, tiles), 0, tiles)
    plan_v[...] = jnp.concatenate(
        [tile_of, sender_y, bin_of, goes_on, live, last, sender_x, last], axis=0
    )
    plan_copy = pltpu.make_async_copy(plan_v, plan, plan_sem)
    plan_copy.start()
    sums[tiles] = jnp.zeros((LANES, LANES), BF16)

    for copy in loads:
        copy.wait()
    for layer in range(LAYERS):
        w_sr[layer, :LANES, :] = turned(identity, raw[0, layer]).astype(BF16)
        w_sr[layer, LANES:, :] = turned(identity, raw[1, layer]).astype(BF16)
        for which, place in ((2, w_edge), (5, w_out)):
            full = turned(identity, raw[which, layer])
            place[layer] = (full - jnp.mean(full, axis=0, keepdims=True)).astype(BF16)
        w_node[layer, :, :LANES] = turned(identity, raw[3, layer]).astype(BF16)
        w_node[layer, :, LANES:] = (
            turned(identity, raw[4, layer]) * edge_g[layer : layer + 1, :]
        ).astype(BF16)
        columns[layer, 0] = spread(edge_b[layer : layer + 1, :])
        columns[layer, 1] = spread(node_b[layer : layer + 1, :])
        columns[layer, 2] = spread(node_g[layer : layer + 1, :])

    def place_tables(layer, pairs, values):
        bias = jnp.concatenate([columns[layer, 0]] * 2, axis=1)
        for pair, value in zip(pairs, values):
            both = dot(w_sr[layer], value)
            sending = both[:LANES].astype(BF16)
            receiving = (both[LANES:] + bias).astype(BF16)
            for n, (i, j) in enumerate(pair):
                part = slice(n * LANES, (n + 1) * LANES)
                tables[layer][j + 1, i + 1] = sending[:, part]
                pr[i * bins_y + j] = receiving[:, part]

    def remote(layer, source, place, device, slot):
        return pltpu.make_async_remote_copy(
            src_ref=tables[layer].at[source],
            dst_ref=tables[layer].at[place],
            send_sem=halo_send.at[layer, slot],
            recv_sem=halo_recv.at[layer, slot],
            device_id=device,
            device_id_type=MESH,
        )

    def column(layer, step_y, row, rows, slot):
        near, far = (1, bins_y + 1) if step_y < 0 else (bins_y, 0)
        cells = pl.ds(1 + row, rows)
        return remote(layer, (near, cells), (far, cells), neighbour(0, step_y), slot)

    def line(layer, step_x):
        near, far = (1, bins_x + 1) if step_x < 0 else (bins_x, 0)
        cells = pl.ds(1, bins_y)
        return remote(layer, (cells, near), (cells, far), neighbour(step_x, 0), 4 + (step_x > 0))

    odd = lax.rem(a, 2)

    def outer_corner(layer, step_y):
        near, far = (1, bins_y + 1) if step_y < 0 else (bins_y, 0)
        source = 1 + (bins_x - 1) * odd
        place = (bins_x + 1) * (1 - odd)
        device = neighbour(2 * odd - 1, step_y)
        return remote(layer, (near, source), (far, place), device, 6 + (step_y > 0))

    def passed_corner(layer, far):
        source = bins_x - (bins_x - 1) * odd
        place = (bins_x + 1) * odd
        device = neighbour(1 - 2 * odd, 0)
        return remote(layer, (far, source), (far, place), device, 8 + (far > 0))

    left, right, low, high = 0, bins_y - 1, 0, bins_x - 1
    middle = [(i, j) for i in range(low + 1, high) for j in range(left + 1, right)]

    def in_pairs(cells):
        return [cells[k : k + 2] for k in range(0, len(cells), 2)]

    def exchange(layer, renew):
        pairs = in_pairs([(low, left), (high, left), (low, right), (high, right)])
        place_tables(layer, pairs, renew(pairs))
        for side, step_y in enumerate((-1, 1)):
            outer_corner(layer, step_y).start()
            column(layer, step_y, low, 1, side).start()
            column(layer, step_y, high, 1, side).start()
        pairs = in_pairs([(i, j) for i in (low, high) for j in range(left + 1, right)])
        pairs += in_pairs([(i, j) for j in (left, right) for i in range(low + 1, high)])
        place_tables(layer, pairs, renew(pairs))
        for step_x in (-1, 1):
            line(layer, step_x).start()
        for side, step_y in enumerate((-1, 1)):
            column(layer, step_y, low + 1, bins_x - 2, 2 + side).start()
        pairs = in_pairs(middle)
        place_tables(layer, pairs, renew(pairs))
        for side, step_y in enumerate((-1, 1)):
            column(layer, step_y, low, 2, side).wait_recv()
        for far in (0, bins_y + 1):
            passed_corner(layer, far).start()

    def halo_waits(layer):
        copies = [line(layer, step_x) for step_x in (-1, 1)]
        copies += [outer_corner(layer, step_y) for step_y in (-1, 1)]
        copies += [passed_corner(layer, far) for far in (0, bins_y + 1)]
        copies += [column(layer, (-1, 1)[side], 1, bins_x - 2, 2 + side) for side in range(2)]
        return copies

    def finish_exchange(layer):
        for copy in halo_waits(layer):
            copy.wait_recv()

    plan_copy.wait()
    for copy in edge_loads:
        copy.wait()

    def mark_tile(p, _):
        t = plan[0, p]
        from_row = es[pl.ds(t, 1), :]
        to_row = jnp.where(plan[4, p] > 0, er[pl.ds(t, 1), :], -1)
        hot[p, :LANES, :] = jnp.where(sub == from_row, 1.0, 0.0).astype(BF16)
        to_hot = jnp.where(sub == to_row, 1.0, 0.0).astype(BF16)
        hot[p, LANES:, :] = to_hot
        hot_n[p] = turned(identity, to_hot).astype(BF16)
        return 0

    lax.fori_loop(0, EARLY, mark_tile, 0, unroll=16)

    def together(table, pair):
        return jnp.concatenate([table[i * bins_y + j] for i, j in pair], axis=1)

    for copy in mig_copies:
        copy.wait()
    for quarter in range(4):
        block = jnp.concatenate([arrived[2 * quarter], arrived[2 * quarter + 1]], axis=0)
        arrived_t[:LANES, quarter * LANES : (quarter + 1) * LANES] = turned(
            identity, block
        ).astype(BF16)
    arrived_t[LANES:, :] = jnp.ones((16, 4 * LANES), BF16)

    def settle(pairs):
        values = []
        for pair in pairs:
            for i, j in pair:
                n = i * bins_y + j
                placed = dot(arrived_t[...], mig_hot[n])
                state[n] = jnp.where(
                    placed[LANES : LANES + 1] > 0.5, placed[:LANES], state[n].astype(F32)
                ).astype(BF16)
            values.append(together(state, pair))
        return values

    exchange(0, settle)
    lax.fori_loop(EARLY, tiles, mark_tile, 0, unroll=16)

    def receivers_of(p, _):
        to_rows[p] = dot(pr[plan[2, p]], hot[p, LANES:, :]).astype(BF16)
        return 0

    def messages(layer):
        table = tables[layer]

        def group(q, total):
            hidden = []
            for g in range(GROUP):
                p = q * GROUP + g
                pre = dot(table[plan[1, p], plan[6, p]], hot[p, :LANES, :])
                hidden.append(jnp.maximum(pre + to_rows[p].astype(F32), 0.0).astype(BF16))
            sent = []
            for g in range(0, GROUP, 2):
                pair = dot(w_edge[layer], jnp.concatenate(hidden[g : g + 2], axis=1))
                var = jnp.mean(pair * pair, axis=0, keepdims=True)
                pair = (pair * lax.rsqrt(var + 1e-5)).astype(BF16)
                sent += [pair[:, :LANES], pair[:, LANES:]]
            for g in range(GROUP):
                p = q * GROUP + g
                total = total * plan[3, p].astype(F32) + dot(sent[g], hot_n[p])
                sums[p] = total.astype(BF16)
            return total

        lax.fori_loop(0, tiles // GROUP, group, jnp.zeros((LANES, LANES), F32))

    def node(layer):
        def renew(pairs):
            bias = jnp.concatenate([columns[layer, 1]] * 2, axis=1)
            gain = jnp.concatenate([columns[layer, 2]] * 2, axis=1)
            hidden = []
            for pair in pairs:
                summed = jnp.concatenate([sums[plan[5, i * bins_y + j]] for i, j in pair], axis=1)
                both = jnp.concatenate([together(state, pair), summed], axis=0)
                pre = dot(w_node[layer], both) + bias
                hidden.append(jnp.maximum(pre, 0.0).astype(BF16))
            values = []
            for pair, value in zip(pairs, hidden):
                z = dot(w_out[layer], value)
                var = jnp.mean(z * z, axis=0, keepdims=True)
                step = z * lax.rsqrt(var + 1e-5) * gain
                values.append((together(state, pair).astype(F32) + step).astype(BF16))
            if layer < LAYERS - 1:
                for pair, value in zip(pairs, values):
                    for n, (i, j) in enumerate(pair):
                        state[i * bins_y + j] = value[:, n * LANES : (n + 1) * LANES]
            return values

        return renew

    for layer in range(LAYERS):
        lax.fori_loop(0, tiles, receivers_of, 0, unroll=16)
        finish_exchange(layer)
        messages(layer)
        if layer < LAYERS - 1:
            exchange(layer + 1, node(layer))
        else:
            renew = node(layer)

            outs = []
            for n in range(bins_x // FINAL):
                pairs = in_pairs(
                    [(FINAL * n + i, j) for i in range(FINAL) for j in range(bins_y)]
                )
                for pair, value in zip(pairs, renew(pairs)):
                    for k, (i, j) in enumerate(pair):
                        part = value[:, k * LANES : (k + 1) * LANES]
                        lat[i, j] = part
                rows = pl.ds(FINAL * n, FINAL)
                outs.append(
                    pltpu.make_async_copy(lat.at[rows], out_ref.at[rows], out_sem.at[n])
                )
                outs[-1].start()
            for copy in outs:
                copy.wait()
    for layer in range(LAYERS):
        for copy in halo_waits(layer):
            copy.wait_send()
        for side, step_y in enumerate((-1, 1)):
            column(layer, step_y, 0, 2, side).wait_send()


def body(*arguments):
    latent, migration, tile_target, tile_offset, tile_count = arguments[:5]
    bins_x, bins_y, slots, features = latent.shape
    tiles = tile_target.shape[2]
    mig = migration.shape[3]
    cells = bins_x * bins_y
    table = (bins_y + 2, bins_x + 2)
    hbm = pl.BlockSpec(memory_space=pl.ANY)
    vmem = pl.BlockSpec(memory_space=pltpu.VMEM)
    smem = pl.BlockSpec(memory_space=pltpu.SMEM)
    block = (LANES, LANES)
    dma = pltpu.SemaphoreType.DMA
    turned_result = pl.pallas_call(
        kernel,
        out_shape=jax.ShapeDtypeStruct(latent.shape, latent.dtype),
        in_specs=[
            hbm, smem, vmem, vmem, vmem, smem, hbm, hbm,
            hbm, hbm, vmem, hbm, vmem, hbm, hbm, vmem, hbm, vmem,
        ],
        out_specs=hbm,
        scratch_shapes=[
            pltpu.VMEM(latent.shape, BF16),
            pltpu.VMEM((cells * slots, features), F32),
            pltpu.VMEM((mig, features), F32),
            pltpu.VMEM((8, mig, features), BF16),
            pltpu.VMEM((8, mig, features), BF16),
            pltpu.VMEM((LANES + 16, 8 * mig), BF16),
            pltpu.VMEM((cells, 8 * mig, LANES), BF16),
            pltpu.VMEM((tiles, LANES), jnp.int32),
            pltpu.VMEM((tiles, LANES), jnp.int32),
            pltpu.VMEM((tiles, 2 * LANES, LANES), BF16),
            pltpu.VMEM((tiles,) + block, BF16),
            pltpu.VMEM((tiles,) + block, BF16),
            pltpu.VMEM(table + block, BF16),
            pltpu.VMEM(table + block, BF16),
            pltpu.VMEM(table + block, BF16),
            pltpu.VMEM((cells,) + block, BF16),
            pltpu.VMEM((tiles + 1,) + block, BF16),
            pltpu.VMEM((cells,) + block, BF16),
            pltpu.VMEM((LAYERS, 2 * LANES, LANES), BF16),
            pltpu.VMEM((LAYERS,) + block, BF16),
            pltpu.VMEM((LAYERS, LANES, 2 * LANES), BF16),
            pltpu.VMEM((LAYERS,) + block, BF16),
            pltpu.VMEM((LAYERS, 3) + block, F32),
            pltpu.VMEM((6, LAYERS) + block, BF16),
            pltpu.VMEM((8, LANES), jnp.int32),
            pltpu.SMEM((8, LANES), jnp.int32),
            dma((9,)),
            dma,
            dma((8,)),
            dma((8,)),
            dma((LAYERS, 10)),
            dma((LAYERS, 10)),
            dma((bins_x,)),
        ],
        compiler_params=pltpu.CompilerParams(
            collective_id=0, has_side_effects=True, vmem_limit_bytes=56 << 20
        ),
        name="particles",
    )(arguments[0], migration, *arguments[1:])
    return jnp.swapaxes(turned_result, 2, 3)


def solution(mesh):
    split = P("gx", "gy")
    in_specs = (split,) * 7 + (P(),) * 10
    return jax.shard_map(
        body, mesh=mesh, in_specs=in_specs, out_specs=split, check_vma=False
    )
```

```python
import jax
import jax.numpy as jnp
from jax import lax
from jax.experimental import pallas as pl
from jax.experimental.pallas import tpu as pltpu
from jax.sharding import PartitionSpec as P

DIRECTIONS = ((-1, -1), (-1, 0), (-1, 1), (0, -1), (0, 1), (1, -1), (1, 0), (1, 1))
MESH = pl.DeviceIdType.MESH
F32 = jnp.float32
BF16 = jnp.bfloat16
LANES = 128
GROUP = 64
LAYERS = 3
EARLY = 64
FINAL = 4


def dot(left, right):
    return jnp.dot(left, right, preferred_element_type=F32)


def turned(identity, block):
    return lax.dot_general(identity, block, (((1,), (1,)), ((), ())), preferred_element_type=F32)


def kernel(
    latent, mig_s, mig_v, target, offset, count, senders, receivers,
    send_w, recv_w, edge_b, edge_w, edge_g, node_w, agg_w, node_b, out_w, node_g,
    out_ref,
    lat, lat32, stage, parcels, arrived, arrived_t, mig_hot,
    es, er, hot, hot_n, to_rows, ps0, ps1, ps2, pr, sums, state,
    w_sr, w_edge, w_node, w_out, columns, raw, plan_v, plan,
    in_sem, plan_sem, mig_send, mig_recv, halo_send, halo_recv, out_sem,
):
    bins_x, bins_y = out_ref.shape[0], out_ref.shape[1]
    tiles = es.shape[0]
    across = bins_x + 2
    tables = (ps0, ps1, ps2)
    a, b = lax.axis_index("gx"), lax.axis_index("gy")
    count_a, count_b = lax.axis_size("gx"), lax.axis_size("gy")

    def neighbour(step_x, step_y):
        return (lax.rem(a + step_x + count_a, count_a), lax.rem(b + step_y + count_b, count_b))

    lat_copy = pltpu.make_async_copy(latent, lat, in_sem.at[0])
    lat_copy.start()
    loads = [
        pltpu.make_async_copy(source, raw.at[which], in_sem.at[1 + which])
        for which, source in enumerate((send_w, recv_w, edge_w, node_w, agg_w, out_w))
    ]
    edge_loads = [
        pltpu.make_async_copy(senders.at[0, 0], es, in_sem.at[7]),
        pltpu.make_async_copy(receivers.at[0, 0], er, in_sem.at[8]),
    ]
    for copy in loads + edge_loads:
        copy.start()

    barrier = pltpu.get_barrier_semaphore()
    for step_x, step_y in DIRECTIONS:
        pl.semaphore_signal(
            barrier, inc=1, device_id=neighbour(step_x, step_y), device_id_type=MESH
        )

    lat_copy.wait()

    def widen(n, _):
        lat32[pl.ds(n * LANES, LANES), :] = lat[n // bins_y, n % bins_y].astype(F32)
        return 0

    lax.fori_loop(0, bins_x * bins_y, widen, 0, unroll=8)

    pl.semaphore_wait(barrier, 8)

    mig = mig_s.shape[3]
    mig_copies = []
    for which in (0, 2, 5, 7, 1, 6, 3, 4):
        step_x, step_y = DIRECTIONS[which]

        def pick(m, _, which=which):
            stage[pl.ds(m, 1), :] = lat32[pl.ds(mig_s[0, 0, which, m], 1), :]
            return 0

        lax.fori_loop(0, mig, pick, 0, unroll=32)
        parcels[which] = stage[...].astype(BF16)
        copy = pltpu.make_async_remote_copy(
            src_ref=parcels.at[which],
            dst_ref=arrived.at[7 - which],
            send_sem=mig_send.at[which],
            recv_sem=mig_recv.at[7 - which],
            device_id=neighbour(step_x, step_y),
            device_id_type=MESH,
        )
        copy.start()
        mig_copies.append(copy)

    sub = lax.broadcasted_iota(jnp.int32, (LANES, LANES), 0)
    lane = lax.broadcasted_iota(jnp.int32, (LANES, LANES), 1)
    identity = jnp.where(sub == lane, 1.0, 0.0).astype(BF16)

    def spread(row):
        return jnp.transpose(jnp.broadcast_to(row, (LANES, LANES)))

    for quarter in range(4):
        row = jnp.concatenate(
            [mig_v[0, 0, 2 * quarter : 2 * quarter + 1, :], mig_v[0, 0, 2 * quarter + 1 : 2 * quarter + 2, :]],
            axis=1,
        ).astype(F32)
        index = spread(row).astype(jnp.int32)

        def mark(n, _, index=index, quarter=quarter):
            mig_hot[n, quarter * LANES : (quarter + 1) * LANES, :] = jnp.where(
                index - n * LANES == lane, 1.0, 0.0
            ).astype(BF16)
            return 0

        lax.fori_loop(0, bins_x * bins_y, mark, 0, unroll=16)

    def turn(n, _):
        state[n] = turned(identity, lat[n // bins_y, n % bins_y]).astype(BF16)
        return 0

    lax.fori_loop(0, bins_x * bins_y, turn, 0, unroll=32)

    lane_row = lax.broadcasted_iota(jnp.int32, (1, LANES), 1)
    bin_row = target[0, 0:1, :]
    off_row = offset[0, 0:1, :]
    step_row = jnp.right_shift(off_row * 11, 5)
    side_row = off_row - 3 * step_row
    sender_row = (jnp.bitwise_and(bin_row, 3) + side_row) * 16 + (
        jnp.right_shift(bin_row, 2) + step_row
    )
    key_row = bin_row * LANES + lane_row
    key_col = spread(key_row)
    packed_col = spread((sender_row * 32 + bin_row) * LANES + lane_row)
    rank = jnp.sum(
        jnp.where(jnp.broadcast_to(key_row, (LANES, LANES)) < key_col, 1, 0),
        axis=1,
        keepdims=True,
    )
    ordered = jnp.sum(jnp.where(rank == lane, packed_col, 0), axis=0, keepdims=True)
    tile_of = jnp.bitwise_and(ordered, LANES - 1)
    bin_of = jnp.bitwise_and(jnp.right_shift(ordered, 7), 31)
    sender_y = jnp.clip(jnp.right_shift(ordered, 16), 0, bins_y + 1)
    sender_x = jnp.clip(jnp.bitwise_and(jnp.right_shift(ordered, 12), 15), 0, across - 1)
    before = pltpu.roll(bin_of, 1, 1)
    goes_on = jnp.where(jnp.logical_and(before == bin_of, lane_row > 0), 1, 0)
    live = jnp.where(tile_of < count[0, 0], 1, 0)
    bin_col = jnp.right_shift(key_col, 7)
    up_to = jnp.sum(jnp.where(bin_col <= lane, 1, 0), axis=0, keepdims=True)
    own = jnp.sum(jnp.where(bin_col == lane, 1, 0), axis=0, keepdims=True)
    last = jnp.clip(jnp.where(own > 0, up_to - 1, tiles), 0, tiles)
    plan_v[...] = jnp.concatenate(
        [tile_of, sender_y, bin_of, goes_on, live, last, sender_x, last], axis=0
    )
    plan_copy = pltpu.make_async_copy(plan_v, plan, plan_sem)
    plan_copy.start()
    sums[tiles] = jnp.zeros((LANES, LANES), BF16)

    for copy in loads:
        copy.wait()
    for layer in range(LAYERS):
        w_sr[layer, :LANES, :] = turned(identity, raw[0, layer]).astype(BF16)
        w_sr[layer, LANES:, :] = turned(identity, raw[1, layer]).astype(BF16)
        for which, place in ((2, w_edge), (5, w_out)):
            full = turned(identity, raw[which, layer])
            place[layer] = (full - jnp.mean(full, axis=0, keepdims=True)).astype(BF16)
        w_node[layer, :, :LANES] = turned(identity, raw[3, layer]).astype(BF16)
        w_node[layer, :, LANES:] = (
            turned(identity, raw[4, layer]) * edge_g[layer : layer + 1, :]
        ).astype(BF16)
        columns[layer, 0] = spread(edge_b[layer : layer + 1, :])
        columns[layer, 1] = spread(node_b[layer : layer + 1, :])
        columns[layer, 2] = spread(node_g[layer : layer + 1, :])

    def place_tables(layer, pairs, values):
        bias = jnp.concatenate([columns[layer, 0]] * 2, axis=1)
        for pair, value in zip(pairs, values):
            both = dot(w_sr[layer], value)
            sending = both[:LANES].astype(BF16)
            receiving = (both[LANES:] + bias).astype(BF16)
            for n, (i, j) in enumerate(pair):
                part = slice(n * LANES, (n + 1) * LANES)
                tables[layer][j + 1, i + 1] = sending[:, part]
                pr[i * bins_y + j] = receiving[:, part]

    def remote(layer, source, place, device, slot):
        return pltpu.make_async_remote_copy(
            src_ref=tables[layer].at[source],
            dst_ref=tables[layer].at[place],
            send_sem=halo_send.at[layer, slot],
            recv_sem=halo_recv.at[layer, slot],
            device_id=device,
            device_id_type=MESH,
        )

    def column(layer, step_y, row, rows, slot):
        near, far = (1, bins_y + 1) if step_y < 0 else (bins_y, 0)
        cells = pl.ds(1 + row, rows)
        return remote(layer, (near, cells), (far, cells), neighbour(0, step_y), slot)

    def line(layer, step_x):
        near, far = (1, bins_x + 1) if step_x < 0 else (bins_x, 0)
        cells = pl.ds(1, bins_y)
        return remote(layer, (cells, near), (cells, far), neighbour(step_x, 0), 4 + (step_x > 0))

    odd = lax.rem(a, 2)

    def outer_corner(layer, step_y):
        near, far = (1, bins_y + 1) if step_y < 0 else (bins_y, 0)
        source = 1 + (bins_x - 1) * odd
        place = (bins_x + 1) * (1 - odd)
        device = neighbour(2 * odd - 1, step_y)
        return remote(layer, (near, source), (far, place), device, 6 + (step_y > 0))

    def passed_corner(layer, far):
        source = bins_x - (bins_x - 1) * odd
        place = (bins_x + 1) * odd
        device = neighbour(1 - 2 * odd, 0)
        return remote(layer, (far, source), (far, place), device, 8 + (far > 0))

    left, right, low, high = 0, bins_y - 1, 0, bins_x - 1
    middle = [(i, j) for i in range(low + 1, high) for j in range(left + 1, right)]

    def in_pairs(cells):
        return [cells[k : k + 2] for k in range(0, len(cells), 2)]

    def exchange(layer, renew):
        pairs = in_pairs([(low, left), (high, left), (low, right), (high, right)])
        place_tables(layer, pairs, renew(pairs))
        for side, step_y in enumerate((-1, 1)):
            outer_corner(layer, step_y).start()
            column(layer, step_y, low, 1, side).start()
            column(layer, step_y, high, 1, side).start()
        pairs = in_pairs([(i, j) for i in (low, high) for j in range(left + 1, right)])
        pairs += in_pairs([(i, j) for j in (left, right) for i in range(low + 1, high)])
        place_tables(layer, pairs, renew(pairs))
        for step_x in (-1, 1):
            line(layer, step_x).start()
        for side, step_y in enumerate((-1, 1)):
            column(layer, step_y, low + 1, bins_x - 2, 2 + side).start()
        pairs = in_pairs(middle)
        place_tables(layer, pairs, renew(pairs))
        for side, step_y in enumerate((-1, 1)):
            column(layer, step_y, low, 2, side).wait_recv()
        for far in (0, bins_y + 1):
            passed_corner(layer, far).start()

    def halo_waits(layer):
        copies = [line(layer, step_x) for step_x in (-1, 1)]
        copies += [outer_corner(layer, step_y) for step_y in (-1, 1)]
        copies += [passed_corner(layer, far) for far in (0, bins_y + 1)]
        copies += [column(layer, (-1, 1)[side], 1, bins_x - 2, 2 + side) for side in range(2)]
        return copies

    def finish_exchange(layer):
        for copy in halo_waits(layer):
            copy.wait_recv()

    plan_copy.wait()
    for copy in edge_loads:
        copy.wait()

    def mark_tile(p, _):
        t = plan[0, p]
        from_row = es[pl.ds(t, 1), :]
        to_row = jnp.where(plan[4, p] > 0, er[pl.ds(t, 1), :], -1)
        hot[p, :LANES, :] = jnp.where(sub == from_row, 1.0, 0.0).astype(BF16)
        to_hot = jnp.where(sub == to_row, 1.0, 0.0).astype(BF16)
        hot[p, LANES:, :] = to_hot
        hot_n[p] = turned(identity, to_hot).astype(BF16)
        return 0

    lax.fori_loop(0, EARLY, mark_tile, 0, unroll=32)

    def together(table, pair):
        return jnp.concatenate([table[i * bins_y + j] for i, j in pair], axis=1)

    for copy in mig_copies:
        copy.wait()
    for quarter in range(4):
        block = jnp.concatenate([arrived[2 * quarter], arrived[2 * quarter + 1]], axis=0)
        arrived_t[:LANES, quarter * LANES : (quarter + 1) * LANES] = turned(
            identity, block
        ).astype(BF16)
    arrived_t[LANES:, :] = jnp.ones((16, 4 * LANES), BF16)

    def settle(pairs):
        values = []
        for pair in pairs:
            for i, j in pair:
                n = i * bins_y + j
                placed = dot(arrived_t[...], mig_hot[n])
                state[n] = jnp.where(
                    placed[LANES : LANES + 1] > 0.5, placed[:LANES], state[n].astype(F32)
                ).astype(BF16)
            values.append(together(state, pair))
        return values

    exchange(0, settle)
    lax.fori_loop(EARLY, tiles, mark_tile, 0, unroll=32)

    def receivers_of(p, _):
        to_rows[p] = dot(pr[plan[2, p]], hot[p, LANES:, :]).astype(BF16)
        return 0

    def messages(layer):
        table = tables[layer]

        def group(q, total):
            hidden = []
            for g in range(GROUP):
                p = q * GROUP + g
                pre = dot(table[plan[1, p], plan[6, p]], hot[p, :LANES, :])
                hidden.append(jnp.maximum(pre + to_rows[p].astype(F32), 0.0).astype(BF16))
            sent = []
            for g in range(0, GROUP, 2):
                pair = dot(w_edge[layer], jnp.concatenate(hidden[g : g + 2], axis=1))
                var = jnp.mean(pair * pair, axis=0, keepdims=True)
                pair = (pair * lax.rsqrt(var + 1e-5)).astype(BF16)
                sent += [pair[:, :LANES], pair[:, LANES:]]
            for g in range(GROUP):
                p = q * GROUP + g
                total = total * plan[3, p].astype(F32) + dot(sent[g], hot_n[p])
                sums[p] = total.astype(BF16)
            return total

        lax.fori_loop(0, tiles // GROUP, group, jnp.zeros((LANES, LANES), F32))

    def node(layer):
        def renew(pairs):
            bias = jnp.concatenate([columns[layer, 1]] * 2, axis=1)
            gain = jnp.concatenate([columns[layer, 2]] * 2, axis=1)
            hidden = []
            for pair in pairs:
                summed = jnp.concatenate([sums[plan[5, i * bins_y + j]] for i, j in pair], axis=1)
                both = jnp.concatenate([together(state, pair), summed], axis=0)
                pre = dot(w_node[layer], both) + bias
                hidden.append(jnp.maximum(pre, 0.0).astype(BF16))
            values = []
            for pair, value in zip(pairs, hidden):
                z = dot(w_out[layer], value)
                var = jnp.mean(z * z, axis=0, keepdims=True)
                step = z * lax.rsqrt(var + 1e-5) * gain
                values.append((together(state, pair).astype(F32) + step).astype(BF16))
            if layer < LAYERS - 1:
                for pair, value in zip(pairs, values):
                    for n, (i, j) in enumerate(pair):
                        state[i * bins_y + j] = value[:, n * LANES : (n + 1) * LANES]
            return values

        return renew

    for layer in range(LAYERS):
        lax.fori_loop(0, tiles, receivers_of, 0, unroll=64)
        finish_exchange(layer)
        messages(layer)
        if layer < LAYERS - 1:
            exchange(layer + 1, node(layer))
        else:
            renew = node(layer)

            outs = []
            for n in range(bins_x // FINAL):
                pairs = in_pairs(
                    [(FINAL * n + i, j) for i in range(FINAL) for j in range(bins_y)]
                )
                for pair, value in zip(pairs, renew(pairs)):
                    for k, (i, j) in enumerate(pair):
                        part = value[:, k * LANES : (k + 1) * LANES]
                        lat[i, j] = part
                rows = pl.ds(FINAL * n, FINAL)
                outs.append(
                    pltpu.make_async_copy(lat.at[rows], out_ref.at[rows], out_sem.at[n])
                )
                outs[-1].start()
            for copy in outs:
                copy.wait()
    for layer in range(LAYERS):
        for copy in halo_waits(layer):
            copy.wait_send()
        for side, step_y in enumerate((-1, 1)):
            column(layer, step_y, 0, 2, side).wait_send()


def body(*arguments):
    latent, migration, tile_target, tile_offset, tile_count = arguments[:5]
    bins_x, bins_y, slots, features = latent.shape
    tiles = tile_target.shape[2]
    mig = migration.shape[3]
    cells = bins_x * bins_y
    table = (bins_y + 2, bins_x + 2)
    hbm = pl.BlockSpec(memory_space=pl.ANY)
    vmem = pl.BlockSpec(memory_space=pltpu.VMEM)
    smem = pl.BlockSpec(memory_space=pltpu.SMEM)
    block = (LANES, LANES)
    dma = pltpu.SemaphoreType.DMA
    turned_result = pl.pallas_call(
        kernel,
        out_shape=jax.ShapeDtypeStruct(latent.shape, latent.dtype),
        in_specs=[
            hbm, smem, vmem, vmem, vmem, smem, hbm, hbm,
            hbm, hbm, vmem, hbm, vmem, hbm, hbm, vmem, hbm, vmem,
        ],
        out_specs=hbm,
        scratch_shapes=[
            pltpu.VMEM(latent.shape, BF16),
            pltpu.VMEM((cells * slots, features), F32),
            pltpu.VMEM((mig, features), F32),
            pltpu.VMEM((8, mig, features), BF16),
            pltpu.VMEM((8, mig, features), BF16),
            pltpu.VMEM((LANES + 16, 8 * mig), BF16),
            pltpu.VMEM((cells, 8 * mig, LANES), BF16),
            pltpu.VMEM((tiles, LANES), jnp.int32),
            pltpu.VMEM((tiles, LANES), jnp.int32),
            pltpu.VMEM((tiles, 2 * LANES, LANES), BF16),
            pltpu.VMEM((tiles,) + block, BF16),
            pltpu.VMEM((tiles,) + block, BF16),
            pltpu.VMEM(table + block, BF16),
            pltpu.VMEM(table + block, BF16),
            pltpu.VMEM(table + block, BF16),
            pltpu.VMEM((cells,) + block, BF16),
            pltpu.VMEM((tiles + 1,) + block, BF16),
            pltpu.VMEM((cells,) + block, BF16),
            pltpu.VMEM((LAYERS, 2 * LANES, LANES), BF16),
            pltpu.VMEM((LAYERS,) + block, BF16),
            pltpu.VMEM((LAYERS, LANES, 2 * LANES), BF16),
            pltpu.VMEM((LAYERS,) + block, BF16),
            pltpu.VMEM((LAYERS, 3) + block, F32),
            pltpu.VMEM((6, LAYERS) + block, BF16),
            pltpu.VMEM((8, LANES), jnp.int32),
            pltpu.SMEM((8, LANES), jnp.int32),
            dma((9,)),
            dma,
            dma((8,)),
            dma((8,)),
            dma((LAYERS, 10)),
            dma((LAYERS, 10)),
            dma((bins_x,)),
        ],
        compiler_params=pltpu.CompilerParams(
            collective_id=0, has_side_effects=True, vmem_limit_bytes=56 << 20
        ),
        name="particles",
    )(arguments[0], migration, *arguments[1:])
    return jnp.swapaxes(turned_result, 2, 3)


def solution(mesh):
    split = P("gx", "gy")
    in_specs = (split,) * 7 + (P(),) * 10
    return jax.shard_map(
        body, mesh=mesh, in_specs=in_specs, out_specs=split, check_vma=False
    )
```

```python
import jax
import jax.numpy as jnp
from jax import lax
from jax.experimental import pallas as pl
from jax.experimental.pallas import tpu as pltpu
from jax.sharding import PartitionSpec as P

DIRECTIONS = ((-1, -1), (-1, 0), (-1, 1), (0, -1), (0, 1), (1, -1), (1, 0), (1, 1))
MESH = pl.DeviceIdType.MESH
F32 = jnp.float32
BF16 = jnp.bfloat16
LANES = 128
GROUP = 64
LAYERS = 3
EARLY = 64
FINAL = 4


def dot(left, right):
    return jnp.dot(left, right, preferred_element_type=F32)


def turned(identity, block):
    return lax.dot_general(identity, block, (((1,), (1,)), ((), ())), preferred_element_type=F32)


def kernel(
    latent, mig_s, mig_v, target, offset, count, senders, receivers,
    send_w, recv_w, edge_b, edge_w, edge_g, node_w, agg_w, node_b, out_w, node_g,
    out_ref,
    lat, lat32, stage, parcels, arrived, arrived_t, mig_hot,
    es, er, hot, hot_n, to_rows, ps0, ps1, ps2, pr, sums, state,
    w_sr, w_edge, w_node, w_out, columns, raw, plan_v, plan,
    in_sem, plan_sem, mig_send, mig_recv, halo_send, halo_recv, out_sem,
):
    bins_x, bins_y = out_ref.shape[0], out_ref.shape[1]
    tiles = es.shape[0]
    across = bins_x + 2
    tables = (ps0, ps1, ps2)
    a, b = lax.axis_index("gx"), lax.axis_index("gy")
    count_a, count_b = lax.axis_size("gx"), lax.axis_size("gy")

    def neighbour(step_x, step_y):
        return (lax.rem(a + step_x + count_a, count_a), lax.rem(b + step_y + count_b, count_b))

    parts = bins_x // 4
    lat_copies = [
        pltpu.make_async_copy(
            latent.at[pl.ds(n * parts, parts)], lat.at[pl.ds(n * parts, parts)], in_sem.at[9 + n]
        )
        for n in range(4)
    ]
    for copy in lat_copies:
        copy.start()
    loads = [
        pltpu.make_async_copy(source, raw.at[which], in_sem.at[1 + which])
        for which, source in enumerate((send_w, recv_w, edge_w, node_w, agg_w, out_w))
    ]
    edge_loads = [
        pltpu.make_async_copy(senders.at[0, 0], es, in_sem.at[7]),
        pltpu.make_async_copy(receivers.at[0, 0], er, in_sem.at[8]),
    ]
    for copy in loads + edge_loads:
        copy.start()

    barrier = pltpu.get_barrier_semaphore()
    for step_x, step_y in DIRECTIONS:
        pl.semaphore_signal(
            barrier, inc=1, device_id=neighbour(step_x, step_y), device_id_type=MESH
        )

    def widen(n, _):
        lat32[pl.ds(n * LANES, LANES), :] = lat[n // bins_y, n % bins_y].astype(F32)
        return 0

    for n, copy in enumerate(lat_copies):
        copy.wait()
        each = parts * bins_y
        lax.fori_loop(n * each, (n + 1) * each, widen, 0, unroll=8)

    pl.semaphore_wait(barrier, 8)

    mig = mig_s.shape[3]
    mig_copies = []
    for which in (0, 2, 5, 7, 1, 6, 3, 4):
        step_x, step_y = DIRECTIONS[which]

        def pick(m, _, which=which):
            stage[pl.ds(m, 1), :] = lat32[pl.ds(mig_s[0, 0, which, m], 1), :]
            return 0

        lax.fori_loop(0, mig, pick, 0, unroll=32)
        parcels[which] = stage[...].astype(BF16)
        copy = pltpu.make_async_remote_copy(
            src_ref=parcels.at[which],
            dst_ref=arrived.at[7 - which],
            send_sem=mig_send.at[which],
            recv_sem=mig_recv.at[7 - which],
            device_id=neighbour(step_x, step_y),
            device_id_type=MESH,
        )
        copy.start()
        mig_copies.append(copy)

    sub = lax.broadcasted_iota(jnp.int32, (LANES, LANES), 0)
    lane = lax.broadcasted_iota(jnp.int32, (LANES, LANES), 1)
    identity = jnp.where(sub == lane, 1.0, 0.0).astype(BF16)

    def spread(row):
        return jnp.transpose(jnp.broadcast_to(row, (LANES, LANES)))

    for quarter in range(4):
        row = jnp.concatenate(
            [mig_v[0, 0, 2 * quarter : 2 * quarter + 1, :], mig_v[0, 0, 2 * quarter + 1 : 2 * quarter + 2, :]],
            axis=1,
        ).astype(F32)
        index = spread(row).astype(jnp.int32)

        def mark(n, _, index=index, quarter=quarter):
            mig_hot[n, quarter * LANES : (quarter + 1) * LANES, :] = jnp.where(
                index - n * LANES == lane, 1.0, 0.0
            ).astype(BF16)
            return 0

        lax.fori_loop(0, bins_x * bins_y, mark, 0, unroll=16)

    def turn(n, _):
        state[n] = turned(identity, lat[n // bins_y, n % bins_y]).astype(BF16)
        return 0

    lax.fori_loop(0, bins_x * bins_y, turn, 0, unroll=32)

    lane_row = lax.broadcasted_iota(jnp.int32, (1, LANES), 1)
    bin_row = target[0, 0:1, :]
    off_row = offset[0, 0:1, :]
    step_row = jnp.right_shift(off_row * 11, 5)
    side_row = off_row - 3 * step_row
    sender_row = (jnp.bitwise_and(bin_row, 3) + side_row) * 16 + (
        jnp.right_shift(bin_row, 2) + step_row
    )
    key_row = bin_row * LANES + lane_row
    key_col = spread(key_row)
    packed_col = spread((sender_row * 32 + bin_row) * LANES + lane_row)
    rank = jnp.sum(
        jnp.where(jnp.broadcast_to(key_row, (LANES, LANES)) < key_col, 1, 0),
        axis=1,
        keepdims=True,
    )
    ordered = jnp.sum(jnp.where(rank == lane, packed_col, 0), axis=0, keepdims=True)
    tile_of = jnp.bitwise_and(ordered, LANES - 1)
    bin_of = jnp.bitwise_and(jnp.right_shift(ordered, 7), 31)
    sender_y = jnp.clip(jnp.right_shift(ordered, 16), 0, bins_y + 1)
    sender_x = jnp.clip(jnp.bitwise_and(jnp.right_shift(ordered, 12), 15), 0, across - 1)
    before = pltpu.roll(bin_of, 1, 1)
    goes_on = jnp.where(jnp.logical_and(before == bin_of, lane_row > 0), 1, 0)
    live = jnp.where(tile_of < count[0, 0], 1, 0)
    bin_col = jnp.right_shift(key_col, 7)
    up_to = jnp.sum(jnp.where(bin_col <= lane, 1, 0), axis=0, keepdims=True)
    own = jnp.sum(jnp.where(bin_col == lane, 1, 0), axis=0, keepdims=True)
    last = jnp.clip(jnp.where(own > 0, up_to - 1, tiles), 0, tiles)
    plan_v[...] = jnp.concatenate(
        [tile_of, sender_y, bin_of, goes_on, live, last, sender_x, last], axis=0
    )
    plan_copy = pltpu.make_async_copy(plan_v, plan, plan_sem)
    plan_copy.start()
    sums[tiles] = jnp.zeros((LANES, LANES), BF16)

    for copy in loads:
        copy.wait()
    for layer in range(LAYERS):
        w_sr[layer, :LANES, :] = turned(identity, raw[0, layer]).astype(BF16)
        w_sr[layer, LANES:, :] = turned(identity, raw[1, layer]).astype(BF16)
        for which, place in ((2, w_edge), (5, w_out)):
            full = turned(identity, raw[which, layer])
            place[layer] = (full - jnp.mean(full, axis=0, keepdims=True)).astype(BF16)
        w_node[layer, :, :LANES] = turned(identity, raw[3, layer]).astype(BF16)
        w_node[layer, :, LANES:] = (
            turned(identity, raw[4, layer]) * edge_g[layer : layer + 1, :]
        ).astype(BF16)
        columns[layer, 0] = spread(edge_b[layer : layer + 1, :])
        columns[layer, 1] = spread(node_b[layer : layer + 1, :])
        columns[layer, 2] = spread(node_g[layer : layer + 1, :])

    def place_tables(layer, pairs, values):
        bias = jnp.concatenate([columns[layer, 0]] * 2, axis=1)
        for pair, value in zip(pairs, values):
            both = dot(w_sr[layer], value)
            sending = both[:LANES].astype(BF16)
            receiving = (both[LANES:] + bias).astype(BF16)
            for n, (i, j) in enumerate(pair):
                part = slice(n * LANES, (n + 1) * LANES)
                tables[layer][j + 1, i + 1] = sending[:, part]
                pr[i * bins_y + j] = receiving[:, part]

    def remote(layer, source, place, device, slot):
        return pltpu.make_async_remote_copy(
            src_ref=tables[layer].at[source],
            dst_ref=tables[layer].at[place],
            send_sem=halo_send.at[layer, slot],
            recv_sem=halo_recv.at[layer, slot],
            device_id=device,
            device_id_type=MESH,
        )

    def column(layer, step_y, row, rows, slot):
        near, far = (1, bins_y + 1) if step_y < 0 else (bins_y, 0)
        cells = pl.ds(1 + row, rows)
        return remote(layer, (near, cells), (far, cells), neighbour(0, step_y), slot)

    def line(layer, step_x):
        near, far = (1, bins_x + 1) if step_x < 0 else (bins_x, 0)
        cells = pl.ds(1, bins_y)
        return remote(layer, (cells, near), (cells, far), neighbour(step_x, 0), 4 + (step_x > 0))

    odd = lax.rem(a, 2)

    def outer_corner(layer, step_y):
        near, far = (1, bins_y + 1) if step_y < 0 else (bins_y, 0)
        source = 1 + (bins_x - 1) * odd
        place = (bins_x + 1) * (1 - odd)
        device = neighbour(2 * odd - 1, step_y)
        return remote(layer, (near, source), (far, place), device, 6 + (step_y > 0))

    def passed_corner(layer, far):
        source = bins_x - (bins_x - 1) * odd
        place = (bins_x + 1) * odd
        device = neighbour(1 - 2 * odd, 0)
        return remote(layer, (far, source), (far, place), device, 8 + (far > 0))

    left, right, low, high = 0, bins_y - 1, 0, bins_x - 1
    middle = [(i, j) for i in range(low + 1, high) for j in range(left + 1, right)]

    def in_pairs(cells):
        return [cells[k : k + 2] for k in range(0, len(cells), 2)]

    def exchange(layer, renew):
        pairs = in_pairs([(low, left), (high, left), (low, right), (high, right)])
        place_tables(layer, pairs, renew(pairs))
        for side, step_y in enumerate((-1, 1)):
            outer_corner(layer, step_y).start()
            column(layer, step_y, low, 1, side).start()
            column(layer, step_y, high, 1, side).start()
        pairs = in_pairs([(i, j) for i in (low, high) for j in range(left + 1, right)])
        pairs += in_pairs([(i, j) for j in (left, right) for i in range(low + 1, high)])
        place_tables(layer, pairs, renew(pairs))
        for step_x in (-1, 1):
            line(layer, step_x).start()
        for side, step_y in enumerate((-1, 1)):
            column(layer, step_y, low + 1, bins_x - 2, 2 + side).start()
        pairs = in_pairs(middle)
        place_tables(layer, pairs, renew(pairs))
        for side, step_y in enumerate((-1, 1)):
            column(layer, step_y, low, 2, side).wait_recv()
        for far in (0, bins_y + 1):
            passed_corner(layer, far).start()

    def halo_waits(layer):
        copies = [line(layer, step_x) for step_x in (-1, 1)]
        copies += [outer_corner(layer, step_y) for step_y in (-1, 1)]
        copies += [passed_corner(layer, far) for far in (0, bins_y + 1)]
        copies += [column(layer, (-1, 1)[side], 1, bins_x - 2, 2 + side) for side in range(2)]
        return copies

    def finish_exchange(layer):
        for copy in halo_waits(layer):
            copy.wait_recv()

    plan_copy.wait()
    for copy in edge_loads:
        copy.wait()

    def mark_tile(p, _):
        t = plan[0, p]
        from_row = es[pl.ds(t, 1), :]
        to_row = jnp.where(plan[4, p] > 0, er[pl.ds(t, 1), :], -1)
        hot[p, :LANES, :] = jnp.where(sub == from_row, 1.0, 0.0).astype(BF16)
        to_hot = jnp.where(sub == to_row, 1.0, 0.0).astype(BF16)
        hot[p, LANES:, :] = to_hot
        hot_n[p] = turned(identity, to_hot).astype(BF16)
        return 0

    lax.fori_loop(0, EARLY, mark_tile, 0, unroll=32)

    def together(table, pair):
        return jnp.concatenate([table[i * bins_y + j] for i, j in pair], axis=1)

    for copy in mig_copies:
        copy.wait()
    for quarter in range(4):
        block = jnp.concatenate([arrived[2 * quarter], arrived[2 * quarter + 1]], axis=0)
        arrived_t[:LANES, quarter * LANES : (quarter + 1) * LANES] = turned(
            identity, block
        ).astype(BF16)
    arrived_t[LANES:, :] = jnp.ones((16, 4 * LANES), BF16)

    def settle(pairs):
        values = []
        for pair in pairs:
            for i, j in pair:
                n = i * bins_y + j
                placed = dot(arrived_t[...], mig_hot[n])
                state[n] = jnp.where(
                    placed[LANES : LANES + 1] > 0.5, placed[:LANES], state[n].astype(F32)
                ).astype(BF16)
            values.append(together(state, pair))
        return values

    exchange(0, settle)
    lax.fori_loop(EARLY, tiles, mark_tile, 0, unroll=32)

    def receivers_of(p, _):
        to_rows[p] = dot(pr[plan[2, p]], hot[p, LANES:, :]).astype(BF16)
        return 0

    def messages(layer):
        table = tables[layer]

        def group(q, total):
            hidden = []
            for g in range(GROUP):
                p = q * GROUP + g
                pre = dot(table[plan[1, p], plan[6, p]], hot[p, :LANES, :])
                hidden.append(jnp.maximum(pre + to_rows[p].astype(F32), 0.0).astype(BF16))
            sent = []
            for g in range(0, GROUP, 2):
                pair = dot(w_edge[layer], jnp.concatenate(hidden[g : g + 2], axis=1))
                var = jnp.mean(pair * pair, axis=0, keepdims=True)
                pair = (pair * lax.rsqrt(var + 1e-5)).astype(BF16)
                sent += [pair[:, :LANES], pair[:, LANES:]]
            for g in range(GROUP):
                p = q * GROUP + g
                total = total * plan[3, p].astype(F32) + dot(sent[g], hot_n[p])
                sums[p] = total.astype(BF16)
            return total

        lax.fori_loop(0, tiles // GROUP, group, jnp.zeros((LANES, LANES), F32))

    def node(layer):
        def renew(pairs):
            bias = jnp.concatenate([columns[layer, 1]] * 2, axis=1)
            gain = jnp.concatenate([columns[layer, 2]] * 2, axis=1)
            hidden = []
            for pair in pairs:
                summed = jnp.concatenate([sums[plan[5, i * bins_y + j]] for i, j in pair], axis=1)
                both = jnp.concatenate([together(state, pair), summed], axis=0)
                pre = dot(w_node[layer], both) + bias
                hidden.append(jnp.maximum(pre, 0.0).astype(BF16))
            values = []
            for pair, value in zip(pairs, hidden):
                z = dot(w_out[layer], value)
                var = jnp.mean(z * z, axis=0, keepdims=True)
                step = z * lax.rsqrt(var + 1e-5) * gain
                values.append((together(state, pair).astype(F32) + step).astype(BF16))
            if layer < LAYERS - 1:
                for pair, value in zip(pairs, values):
                    for n, (i, j) in enumerate(pair):
                        state[i * bins_y + j] = value[:, n * LANES : (n + 1) * LANES]
            return values

        return renew

    for layer in range(LAYERS):
        lax.fori_loop(0, tiles, receivers_of, 0, unroll=64)
        finish_exchange(layer)
        messages(layer)
        if layer < LAYERS - 1:
            exchange(layer + 1, node(layer))
        else:
            renew = node(layer)

            outs = []
            for n in range(bins_x // FINAL):
                pairs = in_pairs(
                    [(FINAL * n + i, j) for i in range(FINAL) for j in range(bins_y)]
                )
                for pair, value in zip(pairs, renew(pairs)):
                    for k, (i, j) in enumerate(pair):
                        part = value[:, k * LANES : (k + 1) * LANES]
                        lat[i, j] = part
                rows = pl.ds(FINAL * n, FINAL)
                outs.append(
                    pltpu.make_async_copy(lat.at[rows], out_ref.at[rows], out_sem.at[n])
                )
                outs[-1].start()
            for past in range(LAYERS):
                for copy in halo_waits(past):
                    copy.wait_send()
                for side, step_y in enumerate((-1, 1)):
                    column(past, step_y, 0, 2, side).wait_send()
            for copy in outs:
                copy.wait()


def body(*arguments):
    latent, migration, tile_target, tile_offset, tile_count = arguments[:5]
    bins_x, bins_y, slots, features = latent.shape
    tiles = tile_target.shape[2]
    mig = migration.shape[3]
    cells = bins_x * bins_y
    table = (bins_y + 2, bins_x + 2)
    hbm = pl.BlockSpec(memory_space=pl.ANY)
    vmem = pl.BlockSpec(memory_space=pltpu.VMEM)
    smem = pl.BlockSpec(memory_space=pltpu.SMEM)
    block = (LANES, LANES)
    dma = pltpu.SemaphoreType.DMA
    turned_result = pl.pallas_call(
        kernel,
        out_shape=jax.ShapeDtypeStruct(latent.shape, latent.dtype),
        in_specs=[
            hbm, smem, vmem, vmem, vmem, smem, hbm, hbm,
            hbm, hbm, vmem, hbm, vmem, hbm, hbm, vmem, hbm, vmem,
        ],
        out_specs=hbm,
        scratch_shapes=[
            pltpu.VMEM(latent.shape, BF16),
            pltpu.VMEM((cells * slots, features), F32),
            pltpu.VMEM((mig, features), F32),
            pltpu.VMEM((8, mig, features), BF16),
            pltpu.VMEM((8, mig, features), BF16),
            pltpu.VMEM((LANES + 16, 8 * mig), BF16),
            pltpu.VMEM((cells, 8 * mig, LANES), BF16),
            pltpu.VMEM((tiles, LANES), jnp.int32),
            pltpu.VMEM((tiles, LANES), jnp.int32),
            pltpu.VMEM((tiles, 2 * LANES, LANES), BF16),
            pltpu.VMEM((tiles,) + block, BF16),
            pltpu.VMEM((tiles,) + block, BF16),
            pltpu.VMEM(table + block, BF16),
            pltpu.VMEM(table + block, BF16),
            pltpu.VMEM(table + block, BF16),
            pltpu.VMEM((cells,) + block, BF16),
            pltpu.VMEM((tiles + 1,) + block, BF16),
            pltpu.VMEM((cells,) + block, BF16),
            pltpu.VMEM((LAYERS, 2 * LANES, LANES), BF16),
            pltpu.VMEM((LAYERS,) + block, BF16),
            pltpu.VMEM((LAYERS, LANES, 2 * LANES), BF16),
            pltpu.VMEM((LAYERS,) + block, BF16),
            pltpu.VMEM((LAYERS, 3) + block, F32),
            pltpu.VMEM((6, LAYERS) + block, BF16),
            pltpu.VMEM((8, LANES), jnp.int32),
            pltpu.SMEM((8, LANES), jnp.int32),
            dma((13,)),
            dma,
            dma((8,)),
            dma((8,)),
            dma((LAYERS, 10)),
            dma((LAYERS, 10)),
            dma((bins_x,)),
        ],
        compiler_params=pltpu.CompilerParams(
            collective_id=0, has_side_effects=True, vmem_limit_bytes=56 << 20
        ),
        name="particles",
    )(arguments[0], migration, *arguments[1:])
    return jnp.swapaxes(turned_result, 2, 3)


def solution(mesh):
    split = P("gx", "gy")
    in_specs = (split,) * 7 + (P(),) * 10
    return jax.shard_map(
        body, mesh=mesh, in_specs=in_specs, out_specs=split, check_vma=False
    )
```
